256 devices in a mesh: ctx: 16 (over y_lo, z), head: 16 (over y_hi, x, core).
Axes of the slice: x: 4, y: 4 (y_hi: 2, y_lo: 2; y = y_hi * 2 + y_lo), z: 8, core: 2. Of those that a mesh axis runs over, the one named last changes fastest.
Arguments:
- q_nope: bfloat16 [2, 1024, 16384], P(None, 'ctx', 'head'), may hold values from -6 to 6
- q_rope: bfloat16 [2, 1024, 8192], P(None, 'ctx', 'head'), may hold values from -8 to 8
- cache_latent: bfloat16 [2, 1024, 576], P(None, 'ctx'), may hold values from -8 to 8
- stretch_latent: bfloat16 [2, 1024, 576], P(None, 'ctx'), may hold values from -6 to 6
- w_uk: bfloat16 [512, 16384], P(None, 'head'), may hold values from -0.25 to 0.25
- w_uv: bfloat16 [512, 16384], P(None, 'head'), may hold values from -0.25 to 0.25
- w_o: bfloat16 [16384, 7168], P('head', 'ctx'), may hold values from -1.1953125 to 1.1953125
- stretch_start: int32 [2], replicated, may hold values from 256 to 1024, as said below
- prompt_len: int32 [2], replicated, may hold values from 512 to 2048, as said below
Outputs:
- mixed: bfloat16 [2, 1024, 7168], P(None, 'head', 'ctx')
The draws below stay inside these ranges and needn't reach their ends.
Inputs may be any that keep to these rules, and one draw needn't show every extreme that they name: `stretch_start`: cached positions before the stretch; some sequence has exactly 1024. `prompt_len`: stretch_start plus the sequence's live stretch positions, which lie between 256 and 1024; some sequence fills both its cache and its stretch.
All inputs are finite; a program needn't handle non-finite values.
Results may differ from the reference program's by a relative error of at most 0.02.
Values may be sent and summed in bfloat16 or wider, within the bound.
No kernel may reach another device: no remote copies, remote signals or barrier semaphores. Data moves between devices by JAX's collectives and lax.ppermute only.
A program may use at most 128 MiB of HBM per device.

```python
import jax
import jax.numpy as jnp
from jax import lax

D = 7168
HEADS = 128
LATENT = 512
ROPE = 64
NOPE = 128
SEQS = 2
STRETCH = 1024
CACHE = 1024


def prompt_bounds(key):
    key_start, key_count, key_full = jax.random.split(key, 3)
    full_seq = jax.random.randint(key_full, (), 0, SEQS)
    chosen = jnp.arange(SEQS) == full_seq
    starts = jnp.where(chosen, CACHE, jax.random.randint(key_start, (SEQS,), CACHE // 4, CACHE + 1))
    counts = jnp.where(chosen, STRETCH, jax.random.randint(key_count, (SEQS,), STRETCH // 4, STRETCH + 1))
    return (starts.astype(jnp.int32), (starts + counts).astype(jnp.int32))


def draw_stretch_start(key, part):
    return prompt_bounds(key)[0]


def draw_prompt_len(key, part):
    return prompt_bounds(key)[1]


def draw_cache_latent(key, part):
    key = jax.random.fold_in(key, 5)
    array_shape = (SEQS, CACHE, LATENT + ROPE)
    return jnp.clip(jax.random.normal(key, array_shape, jnp.float32), -6.0, 6.0).astype(jnp.bfloat16)


def draw_q_rope(key, part):
    key = jax.random.fold_in(key, 7)
    array_shape = (SEQS, STRETCH, HEADS * ROPE)
    return jnp.clip(jax.random.normal(key, array_shape, jnp.float32), -6.0, 6.0).astype(jnp.bfloat16)


def shard_levels(own_key, shape, shards, least, largest):
    def one(dim, blocks):
        heights = jax.random.uniform(jax.random.fold_in(jax.random.fold_in(own_key, 6), dim), (blocks,), jnp.float32, least / len(shards), largest / len(shards))
        return jnp.repeat(jnp.exp(heights), shape[dim] // blocks).reshape((-1,) + (1,) * (len(shape) - dim - 1))

    gain = one(*shards[0])
    for cut in shards[1:]:
        gain = gain * one(*cut)
    return gain


def scatter_about(own_key, extent, deviation, bound, shards=(), kind=jnp.bfloat16):
    array = deviation * jax.random.normal(own_key, extent, jnp.float32)
    if shards:
        array = array * shard_levels(own_key, extent, shards, -0.22, 0.18)
    return jnp.clip(array, -bound, bound).astype(kind)


def setup_inputs(seed: int = 0) -> dict:
    key_list = jax.random.split(jax.random.key(seed), 10)
    q_nope = scatter_about(key_list[0], (SEQS, STRETCH, HEADS * NOPE), 1.0, 6.0, ((1, 16), (2, 16)))
    q_rope = draw_q_rope(jax.random.fold_in(key_list[9], 71), 0)
    cache_latent = draw_cache_latent(jax.random.fold_in(key_list[9], 71), 0)
    stretch_latent = scatter_about(key_list[3], (SEQS, STRETCH, LATENT + ROPE), 1.0, 6.0, ((1, 16),))
    w_uk = scatter_about(key_list[4], (LATENT, HEADS * NOPE), LATENT ** -0.5, 0.25, ((1, 16),))
    w_uv = scatter_about(key_list[5], (LATENT, HEADS * NOPE), LATENT ** -0.5, 0.25, ((1, 16),))
    w_o = scatter_about(key_list[6], (HEADS * NOPE, D), 0.2, 1.1953125, ((0, 16), (1, 16)))
    stretch_start = draw_stretch_start(jax.random.fold_in(key_list[9], 71), 0)
    prompt_len = draw_prompt_len(jax.random.fold_in(key_list[9], 71), 0)
    return dict(q_nope=q_nope, q_rope=q_rope, cache_latent=cache_latent, stretch_latent=stretch_latent, w_uk=w_uk, w_uv=w_uv, w_o=w_o, stretch_start=stretch_start, prompt_len=prompt_len)


neg_fill = -1.0e30
block_heads = 8


def reference(q_nope, q_rope, cache_latent, stretch_latent, w_uk, w_uv, w_o, stretch_start, prompt_len):
    highest = lax.Precision.HIGHEST
    latent = jnp.concatenate([cache_latent, stretch_latent], axis=1)
    compressed = latent[..., :LATENT].astype(jnp.float32)
    rope_keys = latent[..., LATENT:].astype(jnp.float32)
    key_position = jnp.arange(CACHE + STRETCH, dtype=jnp.int32)
    query_position = jnp.arange(STRETCH, dtype=jnp.int32)
    in_cache = key_position[None, None, :] < CACHE
    cache_ok = key_position[None, None, :] < stretch_start[:, None, None]
    stretch_ok = (key_position - CACHE)[None, None, :] <= query_position[None, :, None]
    visible = jnp.where(in_cache, cache_ok, stretch_ok)[:, None]
    score_scale = (NOPE + ROPE) ** -0.5
    span = block_heads * NOPE
    rope_span = block_heads * ROPE

    def one_block(block_index):
        first_col = (block_index * span).astype(jnp.int32)
        first_rope = (block_index * rope_span).astype(jnp.int32)
        up_keys = lax.dynamic_slice_in_dim(w_uk, first_col, span, 1).astype(jnp.float32)
        up_values = lax.dynamic_slice_in_dim(w_uv, first_col, span, 1).astype(jnp.float32)
        key_block = jnp.einsum("skl,lf->skf", compressed, up_keys, precision=highest)
        key_block = key_block.reshape(SEQS, CACHE + STRETCH, block_heads, NOPE)
        value_block = jnp.einsum("skl,lf->skf", compressed, up_values, precision=highest)
        value_block = value_block.reshape(SEQS, CACHE + STRETCH, block_heads, NOPE)
        query_block = lax.dynamic_slice_in_dim(q_nope, first_col, span, 2).astype(jnp.float32)
        query_block = query_block.reshape(SEQS, STRETCH, block_heads, NOPE)
        query_rope = lax.dynamic_slice_in_dim(q_rope, first_rope, rope_span, 2).astype(jnp.float32)
        query_rope = query_rope.reshape(SEQS, STRETCH, block_heads, ROPE)
        scores = jnp.einsum("sqgd,skgd->sgqk", query_block, key_block, precision=highest)
        scores = scores + jnp.einsum("sqge,ske->sgqk", query_rope, rope_keys, precision=highest)
        scores = jnp.where(visible, scores * score_scale, neg_fill)
        row_max = jnp.max(scores, axis=-1, keepdims=True)
        weights = jnp.where(visible, jnp.exp(scores - row_max), 0.0)
        weight_sum = jnp.sum(weights, axis=-1)
        rounded = lax.optimization_barrier(weights.astype(jnp.bfloat16)).astype(jnp.float32)
        heads_out = jnp.einsum("sgqk,skgd->sgqd", rounded, value_block, precision=highest)
        heads_out = heads_out / weight_sum[..., None]
        return heads_out.transpose(0, 2, 1, 3).reshape(SEQS, STRETCH, span)

    blocks = lax.map(one_block, jnp.arange(HEADS // block_heads, dtype=jnp.int32))
    attention = blocks.transpose(1, 2, 0, 3).reshape(SEQS, STRETCH, HEADS * NOPE)
    live_rows = query_position[None, :] < (prompt_len - stretch_start)[:, None]
    attention = jnp.where(live_rows[..., None], attention, 0.0).astype(jnp.bfloat16)
    flat = attention.reshape(SEQS * STRETCH, HEADS * NOPE)
    mixed = jnp.dot(flat, w_o, preferred_element_type=jnp.float32).astype(jnp.bfloat16)
    return mixed.reshape(SEQS, STRETCH, D)
```

```python
import functools

import jax
import jax.numpy as jnp
from jax import lax
from jax.experimental import pallas as pl
from jax.experimental.pallas import tpu as pltpu
from jax.sharding import Mesh, PartitionSpec as P

LATENT = 512
ROPE = 64
NOPE = 128
LOG2E = 1.4426950408889634
HIDDEN = -1e30
GROUP = 4
VMEM_LIMIT = 56 * 1024 * 1024

f32 = jnp.float32
bf16 = jnp.bfloat16


def nt(a, b):
    return lax.dot_general(a, b, (((1,), (1,)), ((), ())), preferred_element_type=f32)


def nn(a, b):
    return jnp.dot(a, b, preferred_element_type=f32)


def attention_kernel(rows, heads, half, scale, *refs):
    info, qn0, qr0, qn1, qr1, wuk, wuv = refs[:7]
    pieces = refs[7:16]
    own, own_lse, message = refs[16:19]
    keys, bias, qaug = refs[19:]
    start, y, z = info[0], info[1], info[2]
    step = 2 * rows
    count = 8 * step
    for d in range(8):
        for part in range(2):
            at = d * step + part * rows
            if d == 4:
                piece = pieces[7 + part][...]
            else:
                piece = pieces[d if d < 4 else d - 1][part * rows : (part + 1) * rows, :]
            keys[at : at + rows, :LATENT] = piece[:, :LATENT]
            rope = piece[:, LATENT:]
            keys[at : at + rows, LATENT:] = jnp.concatenate([rope, rope], axis=1)

    row = lax.broadcasted_iota(jnp.int32, (2 * rows, count), 0)
    col = lax.broadcasted_iota(jnp.int32, (2 * rows, count), 1)
    partner = (row >= rows).astype(jnp.int32)
    q_y = y + partner * (1 - 2 * y)
    q_pos = q_y * half + z * rows + row - partner * rows
    slot = col // step
    k_z = (z - slot) & 7
    inner = col - slot * step
    in_cache = inner < rows
    k_pos = y * half + k_z * rows + jnp.where(in_cache, inner, inner - rows)
    limit = jnp.where(in_cache, start, q_pos + 1)
    bias[...] = jnp.where(k_pos < limit, 0.0, HIDDEN).astype(f32)

    c = scale * LOG2E
    lane = lax.broadcasted_iota(jnp.int32, (2 * rows, 2 * ROPE), 1)
    low = lane < ROPE
    out_lane = lax.broadcasted_iota(jnp.int32, (2 * rows, 128), 1)
    lse_all = jnp.zeros((2 * rows, 128), f32)
    for g in range(heads // GROUP):
        for j in range(GROUP):
            h = g * GROUP + j
            at = h * NOPE
            q = jnp.concatenate([qn0[:, at : at + NOPE], qn1[:, at : at + NOPE]], axis=0)
            r0 = (h // 2) * 2 * ROPE
            r = jnp.concatenate([qr0[:, r0 : r0 + 2 * ROPE], qr1[:, r0 : r0 + 2 * ROPE]], axis=0)
            keep = low if h % 2 == 0 else jnp.logical_not(low)
            base = j * 2 * rows
            qaug[g % 2, base : base + 2 * rows, :LATENT] = nt(q, wuk[:, at : at + NOPE]).astype(bf16)
            qaug[g % 2, base : base + 2 * rows, LATENT:] = jnp.where(keep, r, jnp.zeros_like(r))
        s = nt(qaug[g % 2], keys[...])
        s = (s.reshape(GROUP, 2 * rows, count) + bias[...][None]).reshape(GROUP * 2 * rows, count)
        m = jnp.max(s, axis=-1, keepdims=True)
        p = jnp.exp2((s - m) * c)
        total = jnp.sum(p, axis=-1, keepdims=True)
        acc = nn(p.astype(bf16), keys[:, :LATENT])
        mixed = (acc / total).astype(bf16)
        lse = m * c + jnp.log2(total)
        for j in range(GROUP):
            h = g * GROUP + j
            at = h * NOPE
            base = j * 2 * rows
            o = nn(mixed[base : base + 2 * rows], wuv[:, at : at + NOPE])
            own[:, at : at + NOPE] = o[:rows]
            message[:, at : at + NOPE] = o[rows:].astype(bf16)
            lse_all = jnp.where(out_lane == h, lse[base : base + 2 * rows], lse_all)
    own_lse[...] = lse_all[:rows]
    rest = lse_all[rows:]
    hi = rest.astype(bf16)
    rest = rest - hi.astype(f32)
    mid = rest.astype(bf16)
    low_part = (rest - mid.astype(f32)).astype(bf16)
    wide = heads * NOPE
    message[:, wide : wide + 128] = hi
    message[:, wide + 128 : wide + 256] = mid
    message[:, wide + 256 : wide + 384] = low_part


def attention_part(info, q0, q1, wuk, wuv, pieces, half):
    rows = pieces[0].shape[0] // 2
    heads = wuk.shape[1] // NOPE
    wide = heads * NOPE
    vmem = pl.BlockSpec(memory_space=pltpu.VMEM)
    smem = pl.BlockSpec(memory_space=pltpu.SMEM)
    scale = (NOPE + ROPE) ** -0.5
    return pl.pallas_call(
        functools.partial(attention_kernel, rows, heads, half, scale),
        out_shape=(
            jax.ShapeDtypeStruct((rows, wide), f32),
            jax.ShapeDtypeStruct((rows, 128), f32),
            jax.ShapeDtypeStruct((rows, wide + 384), bf16),
        ),
        in_specs=[smem] + [vmem] * 15,
        out_specs=(vmem, vmem, vmem),
        scratch_shapes=[
            pltpu.VMEM((16 * rows, LATENT + 2 * ROPE), bf16),
            pltpu.VMEM((2 * rows, 16 * rows), f32),
            pltpu.VMEM((2, GROUP * 2 * rows, LATENT + 2 * ROPE), bf16),
        ],
        compiler_params=pltpu.CompilerParams(vmem_limit_bytes=VMEM_LIMIT),
    )(info, q0[0], q0[1], q1[0], q1[1], wuk, wuv, *pieces)


def combine_kernel(rows, heads, info, own_a, lse_a, got_a, own_b, lse_b, got_b, out):
    live = info[3]
    base = info[4]
    wide = heads * NOPE
    alive = base + lax.broadcasted_iota(jnp.int32, (rows, 1), 0) < live
    for part, (own, lse, got) in enumerate(((own_a, lse_a, got_a), (own_b, lse_b, got_b))):
        there = (
            got[:, wide : wide + 128].astype(f32)
            + got[:, wide + 128 : wide + 256].astype(f32)
            + got[:, wide + 256 : wide + 384].astype(f32)
        )
        share = 1.0 / (1.0 + jnp.exp2(there - lse[...]))
        for h in range(heads):
            at = h * NOPE
            w = share[:, h : h + 1]
            o = own[:, at : at + NOPE] * w + got[:, at : at + NOPE].astype(f32) * (1.0 - w)
            out[:, part * wide + at : part * wide + at + NOPE] = jnp.where(alive, o, 0.0).astype(bf16)


def combine(info, a, got_a, b, got_b):
    rows, wide = a[0].shape
    vmem = pl.BlockSpec(memory_space=pltpu.VMEM)
    smem = pl.BlockSpec(memory_space=pltpu.SMEM)
    return pl.pallas_call(
        functools.partial(combine_kernel, rows, wide // NOPE),
        out_shape=jax.ShapeDtypeStruct((rows, 2 * wide), bf16),
        in_specs=[smem] + [vmem] * 6,
        out_specs=vmem,
        compiler_params=pltpu.CompilerParams(vmem_limit_bytes=VMEM_LIMIT),
    )(info, a[0], a[1], got_a, b[0], b[1], got_b)


def project_kernel(rows, info, *refs):
    pieces = refs[:9]
    w00, w01, w10, w11, out, held = refs[9:]
    z = info[2]
    depth = w00.shape[0]
    for d in range(8):
        if d == 4:
            held[d * rows : d * rows + rows // 2, :] = pieces[7][...]
            held[d * rows + rows // 2 : (d + 1) * rows, :] = pieces[8][...]
        else:
            held[d * rows : (d + 1) * rows, :] = pieces[d if d < 4 else d - 1][...]
    left = held[:, :depth]
    right = held[:, depth:]
    first = nn(left, w00[...]) + nn(right, w10[...])
    second = nn(left, w01[...]) + nn(right, w11[...])
    both = jnp.concatenate([first, second], axis=1).astype(bf16)
    for d in range(8):
        out[(z - d) & 7] = both[d * rows : (d + 1) * rows]


def project(info, pieces, w00, w01, w10, w11):
    rows, wide = pieces[0].shape
    vmem = pl.BlockSpec(memory_space=pltpu.VMEM)
    smem = pl.BlockSpec(memory_space=pltpu.SMEM)
    return pl.pallas_call(
        functools.partial(project_kernel, rows),
        out_shape=jax.ShapeDtypeStruct((8, rows, 2 * w00.shape[1]), bf16),
        in_specs=[smem] + [vmem] * 13,
        out_specs=vmem,
        scratch_shapes=[pltpu.VMEM((8 * rows, wide), bf16)],
        compiler_params=pltpu.CompilerParams(vmem_limit_bytes=VMEM_LIMIT),
    )(info, *pieces, w00, w01, w10, w11)


def swap(x, axis):
    return lax.ppermute(x, axis, [(0, 1), (1, 0)])


def ring(x):
    up = [(i, (i + 1) % 8) for i in range(8)]
    down = [(i, (i - 1) % 8) for i in range(8)]
    a = b = x
    ups, downs = [], []
    for _ in range(3):
        a = lax.ppermute(a, "z", up)
        b = lax.ppermute(b, "z", down)
        ups.append(a)
        downs.append(b)
    cut = x.shape[0] // 2
    first = lax.ppermute(a[:cut], "z", up)
    second = lax.ppermute(b[cut:], "z", down)
    return [x] + ups + downs[::-1] + [first, second]


def local(q_nope, q_rope, cache_latent, stretch_latent, w_uk, w_uv, w_o, stretch_start, prompt_len):
    rows = q_nope.shape[1]
    core = lax.axis_index("core")
    y = lax.axis_index("yl")
    yh = lax.axis_index("yh")
    z = lax.axis_index("z")
    half = 8 * rows
    wide_q = q_nope.shape[2]

    def mine(x):
        return lax.dynamic_index_in_dim(x, core, 0, keepdims=False)

    def other(x):
        return lax.dynamic_index_in_dim(x, 1 - core, 0, keepdims=False)

    info = jnp.stack(
        [mine(stretch_start), y, z, mine(prompt_len) - mine(stretch_start), y * half + z * rows]
    ).astype(jnp.int32)

    pieces = ring(jnp.concatenate([mine(cache_latent), mine(stretch_latent)], axis=0))

    q_own = jnp.concatenate([mine(q_nope), mine(q_rope)], axis=1)
    q_sent = jnp.concatenate([other(q_nope), other(q_rope)], axis=1)
    q_here = jnp.stack([q_own, swap(q_sent, "core")])
    q_there = swap(q_here, "yl")
    w_uk2 = swap(w_uk, "core")
    w_uv2 = swap(w_uv, "core")
    w_o_y = swap(w_o, "yl")
    w_o_c = swap(w_o, "core")
    w_o_cy = swap(w_o_y, "core")

    def split(x):
        return (x[:, :wide_q], x[:, wide_q:])

    a = attention_part(info, split(q_here[0]), split(q_there[0]), w_uk, w_uv, pieces, half)
    got_a = swap(a[2], "yl")
    b = attention_part(info, split(q_here[1]), split(q_there[1]), w_uk2, w_uv2, pieces, half)
    got_b = swap(b[2], "yl")
    attention = combine(info, a, got_a, b, got_b)

    partial = project(info, ring(attention), w_o, w_o_y, w_o_c, w_o_cy)
    parts = lax.all_to_all(partial, ("x", "core"), 0, 0, tiled=True)
    cols = w_o.shape[1]
    summed = jnp.sum(parts.reshape(4, 2, rows, 2 * cols).astype(f32), axis=0).astype(bf16)
    by_col = (summed[:, :, :cols], summed[:, :, cols:])
    same = yh == y
    keep = jnp.where(same, by_col[0], by_col[1])
    move = jnp.where(same, by_col[1], by_col[0])
    got = lax.ppermute(keep, ("yl", "yh"), [(0, 0), (1, 2), (2, 1), (3, 3)])
    got2 = lax.ppermute(move, ("yl", "yh"), [(0, 2), (2, 3), (1, 0), (3, 1)])
    return (got.astype(f32) + got2.astype(f32)).astype(bf16)


def solution(mesh):
    fine = Mesh(mesh.devices.reshape(2, 8, 2, 4, 2), ("yl", "z", "yh", "x", "core"))
    ctx = ("yl", "z")
    head = ("yh", "x", "core")
    placed = (
        P(None, ctx, head),
        P(None, ctx, head),
        P(None, ctx, None),
        P(None, ctx, None),
        P(None, head),
        P(None, head),
        P(head, ctx),
        P(),
        P(),
    )
    return jax.shard_map(
        local, mesh=fine, in_specs=placed, out_specs=P(None, head, ctx), check_vma=False
    )
```

```python
import functools

import jax
import jax.numpy as jnp
from jax import lax
from jax.experimental import pallas as pl
from jax.experimental.pallas import tpu as pltpu
from jax.sharding import Mesh, PartitionSpec as P

LATENT = 512
ROPE = 64
NOPE = 128
LOG2E = 1.4426950408889634
HIDDEN = -1e30
GROUP = 4
MIB = 1024 * 1024

f32 = jnp.float32
bf16 = jnp.bfloat16


def nt(a, b):
    return lax.dot_general(a, b, (((1,), (1,)), ((), ())), preferred_element_type=f32)


def nn(a, b):
    return jnp.dot(a, b, preferred_element_type=f32)


def attention_kernel(rows, heads, half, scale, *refs):
    coords, starts, q0, q1, wuk, wuv = refs[:6]
    pieces = refs[6:15]
    own, own_lse, message = refs[16:19]
    keys, bias, qaug = refs[19:]
    y, z, core = coords[0], coords[1], coords[2]
    start = starts[core]
    step = 2 * rows
    count = 8 * step
    wide = heads * NOPE
    for d in range(8):
        for part in range(2):
            at = d * step + part * rows
            if d == 4:
                piece = pieces[7 + part][...]
            else:
                piece = pieces[d if d < 4 else d - 1][part * rows : (part + 1) * rows, :]
            keys[at : at + rows, :LATENT] = piece[:, :LATENT]
            rope = piece[:, LATENT:]
            keys[at : at + rows, LATENT:] = jnp.concatenate([rope, rope], axis=1)

    row = lax.broadcasted_iota(jnp.int32, (2 * rows, count), 0)
    col = lax.broadcasted_iota(jnp.int32, (2 * rows, count), 1)
    partner = (row >= rows).astype(jnp.int32)
    q_y = y + partner * (1 - 2 * y)
    q_pos = q_y * half + z * rows + row - partner * rows
    slot = col // step
    k_z = (z - slot) & 7
    inner = col - slot * step
    in_cache = inner < rows
    k_pos = y * half + k_z * rows + jnp.where(in_cache, inner, inner - rows)
    limit = jnp.where(in_cache, start, q_pos + 1)
    bias[...] = jnp.where(k_pos < limit, 0.0, HIDDEN).astype(f32)

    c = scale * LOG2E
    lane = lax.broadcasted_iota(jnp.int32, (2 * rows, 2 * ROPE), 1)
    low = lane < ROPE
    out_lane = lax.broadcasted_iota(jnp.int32, (2 * rows, 128), 1)
    lse_all = jnp.zeros((2 * rows, 128), f32)
    for g in range(heads // GROUP):
        for j in range(GROUP):
            h = g * GROUP + j
            at = h * NOPE
            q = jnp.concatenate([q0[:, at : at + NOPE], q1[:, at : at + NOPE]], axis=0)
            r0 = wide + (h // 2) * 2 * ROPE
            r = jnp.concatenate([q0[:, r0 : r0 + 2 * ROPE], q1[:, r0 : r0 + 2 * ROPE]], axis=0)
            keep = low if h % 2 == 0 else jnp.logical_not(low)
            base = j * 2 * rows
            qaug[g % 2, base : base + 2 * rows, :LATENT] = nt(q, wuk[:, at : at + NOPE]).astype(bf16)
            qaug[g % 2, base : base + 2 * rows, LATENT:] = jnp.where(keep, r, jnp.zeros_like(r))
        s = nt(qaug[g % 2], keys[...])
        s = (s.reshape(GROUP, 2 * rows, count) + bias[...][None]).reshape(GROUP * 2 * rows, count)
        m = jnp.max(s, axis=-1, keepdims=True)
        p = jnp.exp2((s - m) * c)
        total = jnp.sum(p, axis=-1, keepdims=True)
        acc = nn(p.astype(bf16), keys[:, :LATENT])
        mixed = (acc / total).astype(bf16)
        lse = m * c + jnp.log2(total)
        for j in range(GROUP):
            h = g * GROUP + j
            at = h * NOPE
            base = j * 2 * rows
            o = nn(mixed[base : base + 2 * rows], wuv[:, at : at + NOPE])
            own[:, at : at + NOPE] = o[:rows]
            message[:, at : at + NOPE] = o[rows:].astype(bf16)
            lse_all = jnp.where(out_lane == h, lse[base : base + 2 * rows], lse_all)
    own_lse[...] = lse_all[:rows]
    rest = lse_all[rows:]
    hi = rest.astype(bf16)
    rest = rest - hi.astype(f32)
    mid = rest.astype(bf16)
    last = (rest - mid.astype(f32)).astype(bf16)
    message[:, wide : wide + 128] = hi
    message[:, wide + 128 : wide + 256] = mid
    message[:, wide + 256 : wide + 384] = last


VMEM = pl.BlockSpec(memory_space=pltpu.VMEM)
SMEM = pl.BlockSpec(memory_space=pltpu.SMEM)
ANY = pl.BlockSpec(memory_space=pl.ANY)


def params(mib):
    return pltpu.CompilerParams(vmem_limit_bytes=mib * MIB)


def held_in_vmem(*arrays):
    return tuple(pltpu.with_memory_space_constraint(x, pltpu.VMEM) for x in arrays)


def cost(flops, exps=0):
    return pl.CostEstimate(flops=flops, transcendentals=exps, bytes_accessed=4 * MIB)


def attention_part(coords, starts, q0, q1, wuk, wuv, pieces, half, earlier):
    rows = pieces[0].shape[0] // 2
    heads = wuk.shape[1] // NOPE
    wide = heads * NOPE
    scale = (NOPE + ROPE) ** -0.5
    return pl.pallas_call(
        functools.partial(attention_kernel, rows, heads, half, scale),
        out_shape=(
            pltpu.VMEM((rows, wide), f32),
            pltpu.VMEM((rows, 128), f32),
            pltpu.VMEM((rows, wide + 384), bf16),
        ),
        in_specs=[SMEM, SMEM] + [VMEM] * 13 + [ANY],
        out_specs=(VMEM, VMEM, VMEM),
        scratch_shapes=[
            pltpu.VMEM((16 * rows, LATENT + 2 * ROPE), bf16),
            pltpu.VMEM((2 * rows, 16 * rows), f32),
            pltpu.VMEM((2, GROUP * 2 * rows, LATENT + 2 * ROPE), bf16),
        ],
        compiler_params=params(24),
        cost_estimate=cost(
            2 * heads * 2 * rows * 16 * rows * (2 * LATENT + 2 * ROPE), heads * 32 * rows * rows
        ),
    )(coords, starts, *held_in_vmem(q0, q1, wuk, wuv, *pieces, earlier))


def combine_kernel(rows, heads, half, coords, starts, lens, *refs):
    weights, out, copied, sem = refs[6:]
    moving = pltpu.make_async_copy(weights, copied, sem)
    moving.start()
    y, z, core = coords[0], coords[1], coords[2]
    live = lens[core] - starts[core]
    base = y * half + z * rows
    wide = heads * NOPE
    alive = base + lax.broadcasted_iota(jnp.int32, (rows, 1), 0) < live
    for part in range(2):
        own, lse, got = refs[3 * part : 3 * part + 3]
        there = (
            got[:, wide : wide + 128].astype(f32)
            + got[:, wide + 128 : wide + 256].astype(f32)
            + got[:, wide + 256 : wide + 384].astype(f32)
        )
        share = 1.0 / (1.0 + jnp.exp2(there - lse[...]))
        for h in range(heads):
            at = h * NOPE
            w = share[:, h : h + 1]
            o = own[:, at : at + NOPE] * w + got[:, at : at + NOPE].astype(f32) * (1.0 - w)
            at = part * wide + h * NOPE
            out[:, at : at + NOPE] = jnp.where(alive, o, 0.0).astype(bf16)
    moving.wait()


def combine(coords, starts, lens, parts, weights, half):
    rows, wide = parts[0].shape
    return pl.pallas_call(
        functools.partial(combine_kernel, rows, wide // NOPE, half),
        out_shape=(
            pltpu.VMEM((rows, 2 * wide), bf16),
            pltpu.VMEM(weights.shape, weights.dtype),
        ),
        in_specs=[SMEM, SMEM, SMEM] + [VMEM] * 6 + [ANY],
        out_specs=(VMEM, ANY),
        scratch_shapes=[pltpu.SemaphoreType.DMA(())],
        compiler_params=params(4),
    )(coords, starts, lens, *held_in_vmem(*parts), weights)


def project_kernel(rows, at, extra, *refs):
    coords = refs[0]
    count = len(at)
    pieces = refs[1 : 1 + count]
    w00, w01, w10, w11 = refs[1 + count : 5 + count]
    out, held = refs[5 + count + extra :]
    z, same = coords[1], coords[3]
    depth = w00.shape[1]
    place, slots = 0, []
    for piece, slot in zip(pieces, at):
        held[place : place + piece.shape[0], :] = piece[...]
        if slot is not None:
            slots.append((slot, place))
        place += piece.shape[0]
    left = held[:, :depth]
    right = held[:, depth:]
    mine = nt(left, w00[...]) + nt(right, w10[...])
    other = nt(left, w01[...]) + nt(right, w11[...])
    swapped = same == 0
    both = jnp.concatenate(
        [jnp.where(swapped, other, mine), jnp.where(swapped, mine, other)], axis=1
    ).astype(bf16)
    for slot, place in slots:
        out[(z - slot) & 7] = both[place : place + rows]


def project(coords, rows, pieces, at, weights, before=None):
    wide = pieces[0].shape[1]
    cols = weights[0].shape[0]
    total = sum(p.shape[0] for p in pieces)
    extra = 0 if before is None else 1
    inputs = held_in_vmem(*pieces, *weights)
    if extra:
        inputs += held_in_vmem(before)
    return pl.pallas_call(
        functools.partial(project_kernel, rows, at, extra),
        out_shape=pltpu.VMEM((8, rows, 2 * cols), bf16),
        in_specs=[SMEM] + [VMEM] * (len(pieces) + 4) + [ANY] * extra,
        out_specs=VMEM,
        scratch_shapes=[pltpu.VMEM((total, wide), bf16)],
        input_output_aliases={5 + len(pieces): 0} if extra else {},
        compiler_params=params(12),
        cost_estimate=cost(4 * total * wide * cols),
    )(coords, *inputs)


def level_kernel(*refs):
    pass


def level(arrays, earlier=()):
    count = len(arrays)
    return pl.pallas_call(
        level_kernel,
        out_shape=tuple(pltpu.VMEM(x.shape, x.dtype) for x in arrays),
        in_specs=[ANY] * (count + len(earlier)),
        out_specs=(ANY,) * count,
        input_output_aliases={i: i for i in range(count)},
        compiler_params=params(1),
    )(*held_in_vmem(*arrays, *earlier))


def swap(x, axis):
    return lax.ppermute(x, axis, [(0, 1), (1, 0)])


UP = [(i, (i + 1) % 8) for i in range(8)]
DOWN = [(i, (i - 1) % 8) for i in range(8)]


def step(a, b):
    return lax.ppermute(a, "z", UP), lax.ppermute(b, "z", DOWN)


def last(a, b):
    cut = a.shape[0] // 2
    return step(a[:cut], b[cut:])


def in_order(x, ups, downs, ends):
    return [x, *ups, *downs[::-1], *ends]


def local(q_nope, q_rope, cache_latent, stretch_latent, w_uk, w_uv, w_o, stretch_start, prompt_len):
    rows = q_nope.shape[1]
    core = lax.axis_index("core")
    y = lax.axis_index("yl")
    yh = lax.axis_index("yh")
    z = lax.axis_index("z")
    half = 8 * rows
    coords = jnp.stack([y, z, core, (yh == y).astype(jnp.int32)])

    def mine(x):
        return lax.dynamic_index_in_dim(x, core, 0, keepdims=False)

    def other(x):
        return lax.dynamic_index_in_dim(x, 1 - core, 0, keepdims=False)

    latent = jnp.concatenate([mine(cache_latent), mine(stretch_latent)], axis=0)
    q_own = jnp.concatenate([mine(q_nope), mine(q_rope)], axis=1)
    q_sent = jnp.concatenate([other(q_nope), other(q_rope)], axis=1)
    u1, d1 = level(step(latent, latent))
    q_own_y = swap(q_own, "yl")
    q_got = swap(q_sent, "core")
    u2, d2, q_got = level((*step(u1, d1), q_got), (q_own_y,))
    q_got_y = swap(q_got, "yl")
    w_uk2 = swap(w_uk, "core")
    w_uv2 = swap(w_uv, "core")
    u3, d3 = level(step(u2, d2), (q_got_y, w_uk2, w_uv2))
    pieces = in_order(latent, (u1, u2, u3), (d1, d2, d3), last(u3, d3))

    a = attention_part(
        coords, stretch_start, q_own, q_own_y, w_uk, w_uv, pieces, half, u1
    )
    b = attention_part(coords, stretch_start, q_got, q_got_y, w_uk2, w_uv2, pieces, half, a[1])
    parts = (*a[:2], swap(a[2], "yl"), *b[:2], swap(b[2], "yl"))
    attention, w_t = combine(coords, stretch_start, prompt_len, parts, w_o.T, half)
    u1, d1 = level(step(attention, attention))
    w_t_c = swap(w_t, "core")
    w_t_y = swap(w_t, "yl")
    u2, d2 = level(step(u1, d1), (w_t_c,))
    u3, d3, w_t_y = level((*step(u2, d2), w_t_y))
    w_t_cy = swap(w_t_y, "core")
    rounds = in_order(attention, (u1, u2, u3), (d1, d2, d3), last(u3, d3))
    weights = (w_t, w_t_y, w_t_c, w_t_cy)

    early, late = (0, 1, 2, 6, 7), (3, 5, 4, None)
    before = project(coords, rows, [rounds[i if i < 4 else i - 1] for i in early], early, weights)
    partial = project(
        coords, rows, [rounds[3], rounds[4], rounds[7], rounds[8]], late, weights, before
    )
    parts = lax.all_to_all(partial, ("x", "core"), 0, 0, tiled=True)
    cols = w_o.shape[1]
    summed = jnp.sum(parts.reshape(4, 2, rows, 2 * cols).astype(f32), axis=0).astype(bf16)
    got = lax.ppermute(summed[:, :, :cols], ("yl", "yh"), [(0, 0), (1, 2), (2, 1), (3, 3)])
    got2 = lax.ppermute(summed[:, :, cols:], ("yl", "yh"), [(0, 2), (2, 3), (1, 0), (3, 1)])
    return (got.astype(f32) + got2.astype(f32)).astype(bf16)


def solution(mesh):
    fine = Mesh(mesh.devices.reshape(2, 8, 2, 4, 2), ("yl", "z", "yh", "x", "core"))
    ctx = ("yl", "z")
    head = ("yh", "x", "core")
    placed = (
        P(None, ctx, head),
        P(None, ctx, head),
        P(None, ctx, None),
        P(None, ctx, None),
        P(None, head),
        P(None, head),
        P(head, ctx),
        P(),
        P(),
    )
    return jax.shard_map(
        local, mesh=fine, in_specs=placed, out_specs=P(None, head, ctx), check_vma=False
    )
```

```python
import functools

import jax
import jax.numpy as jnp
from jax import lax
from jax.experimental import pallas as pl
from jax.experimental.pallas import tpu as pltpu
from jax.sharding import Mesh, PartitionSpec as P

LATENT = 512
ROPE = 64
NOPE = 128
LOG2E = 1.4426950408889634
HIDDEN = -1e30
GROUP = 8
MIB = 1024 * 1024

f32 = jnp.float32
bf16 = jnp.bfloat16


def nt(a, b):
    return lax.dot_general(a, b, (((1,), (1,)), ((), ())), preferred_element_type=f32)


def nn(a, b):
    return jnp.dot(a, b, preferred_element_type=f32)


def load_keys(rows, slots, pieces, keys):
    place = 0
    for piece in pieces:
        height = piece.shape[0]
        value = piece[...]
        keys[place : place + height, :LATENT] = value[:, :LATENT]
        rope = value[:, LATENT:]
        keys[place : place + height, LATENT:] = jnp.concatenate([rope, rope], axis=1)
        place += height


def hidden_keys(rows, slots, half, starts):
    y, z = lax.axis_index("yl"), lax.axis_index("z")
    start = starts[lax.axis_index("core")]
    row = lax.broadcasted_iota(jnp.int32, (2 * rows, 2 * rows), 0)
    col = lax.broadcasted_iota(jnp.int32, (2 * rows, 2 * rows), 1)
    partner = (row >= rows).astype(jnp.int32)
    q_y = y + partner * (1 - 2 * y)
    q_pos = q_y * half + z * rows + row - partner * rows
    in_cache = col < rows
    limit = jnp.where(in_cache, start, q_pos + 1)
    inner = y * half + jnp.where(in_cache, col, col - rows)
    return jnp.concatenate(
        [
            jnp.where(inner + ((z - d) & 7) * rows < limit, 0.0, HIDDEN).astype(f32)
            for d in slots
        ],
        axis=1,
    )


def scores_of(q, keys, bias):
    s = nt(q, keys[...])
    height, count = bias.shape
    return (s.reshape(GROUP, height, count) + bias[...][None]).reshape(GROUP * height, count)


def tiled(x, like):
    return jnp.concatenate([x] * (like.shape[1] // 128), axis=1)


def first_kernel(rows, heads, half, slots, *refs):
    c = (NOPE + ROPE) ** -0.5 * LOG2E
    starts, q0, q1, wuk = refs[:4]
    pieces = refs[4 : 4 + len(slots)]
    qaug, acc, stats, keys, bias = refs[5 + len(slots) :]
    load_keys(rows, slots, pieces, keys)
    bias[...] = hidden_keys(rows, slots, half, starts)
    wide = heads * NOPE
    block = GROUP * 2 * rows
    low = lax.broadcasted_iota(jnp.int32, (2 * rows, 2 * ROPE), 1) < ROPE
    for g in range(heads // GROUP):
        for j in range(GROUP):
            h = g * GROUP + j
            at = h * NOPE
            q = jnp.concatenate([q0[:, at : at + NOPE], q1[:, at : at + NOPE]], axis=0)
            r0 = wide + (h // 2) * 2 * ROPE
            r = jnp.concatenate([q0[:, r0 : r0 + 2 * ROPE], q1[:, r0 : r0 + 2 * ROPE]], axis=0)
            keep = low if h % 2 == 0 else jnp.logical_not(low)
            base = h * 2 * rows
            qaug[base : base + 2 * rows, :LATENT] = nt(q, wuk[:, at : at + NOPE]).astype(bf16)
            qaug[base : base + 2 * rows, LATENT:] = jnp.where(keep, r, jnp.zeros_like(r))
        here = slice(g * block, (g + 1) * block)
        s = scores_of(qaug[here], keys, bias)
        m = jnp.broadcast_to(jnp.max(s, axis=-1, keepdims=True), (block, 128))
        p = jnp.exp2((s - tiled(m, s)) * c)
        acc[here] = nn(p.astype(bf16), keys[:, :LATENT])
        stats[here, :128] = m
        stats[here, 128:] = jnp.broadcast_to(jnp.sum(p, axis=-1, keepdims=True), (block, 128))


def second_kernel(rows, heads, half, slots, *refs):
    c = (NOPE + ROPE) ** -0.5 * LOG2E
    starts, qaug, acc, stats, wuv = refs[:5]
    count = len(refs) - 11
    pieces = refs[5 : 5 + count]
    own, own_lse, message, keys, bias = refs[6 + count :]
    load_keys(rows, slots, pieces, keys)
    bias[...] = hidden_keys(rows, slots, half, starts)
    wide = heads * NOPE
    block = GROUP * 2 * rows
    out_lane = lax.broadcasted_iota(jnp.int32, (rows, 128), 1)
    own_all = jnp.zeros((rows, 128), f32)
    sent_all = jnp.zeros((rows, 128), f32)
    for g in range(heads // GROUP):
        here = slice(g * block, (g + 1) * block)
        s = scores_of(qaug[here], keys, bias)
        m1 = stats[here, :128]
        m = jnp.maximum(m1, jnp.max(s, axis=-1, keepdims=True))
        factor = jnp.exp2((m1 - m) * c)
        p = jnp.exp2((s - tiled(m, s)) * c)
        total = stats[here, 128:] * factor + jnp.sum(p, axis=-1, keepdims=True)
        fresh = nn(p.astype(bf16), keys[:, :LATENT])
        inverse = 1.0 / total
        mixed = acc[here] * tiled(factor * inverse, fresh) + fresh * tiled(inverse, fresh)
        mixed = mixed.astype(bf16)
        lse = m * c + jnp.log2(total)
        for j in range(GROUP):
            h = g * GROUP + j
            at = h * NOPE
            base = j * 2 * rows
            o = nn(mixed[base : base + 2 * rows], wuv[:, at : at + NOPE])
            own[:, at : at + NOPE] = o[:rows]
            message[:, at : at + NOPE] = o[rows:].astype(bf16)
            own_all = jnp.where(out_lane == h, lse[base : base + rows], own_all)
            rest = lse[base + rows : base + 2 * rows]
            for term in range(3):
                part = rest.astype(bf16).astype(f32)
                sent_all = jnp.where(out_lane == term * heads + h, part, sent_all)
                rest = rest - part
    own_lse[...] = own_all
    message[:, wide : wide + 128] = sent_all.astype(bf16)


VMEM = pl.BlockSpec(memory_space=pltpu.VMEM)
SMEM = pl.BlockSpec(memory_space=pltpu.SMEM)
ANY = pl.BlockSpec(memory_space=pl.ANY)


def params(mib):
    return pltpu.CompilerParams(vmem_limit_bytes=mib * MIB)


def held_in_vmem(*arrays):
    return tuple(pltpu.with_memory_space_constraint(x, pltpu.VMEM) for x in arrays)


def in_hbm(*arrays):
    return tuple(pltpu.with_memory_space_constraint(x, pltpu.HBM) for x in arrays)


def cost(flops, exps=0):
    return pl.CostEstimate(flops=flops, transcendentals=exps, bytes_accessed=4 * MIB)


def attention_first(starts, q0, q1, wuk, pieces, slots, half, earlier):
    rows = q0.shape[0]
    heads = wuk.shape[1] // NOPE
    height = heads * 2 * rows
    count = 2 * rows * len(slots)
    return pl.pallas_call(
        functools.partial(first_kernel, rows, heads, half, slots),
        out_shape=(
            pltpu.VMEM((height, LATENT + 2 * ROPE), bf16),
            pltpu.VMEM((height, LATENT), f32),
            pltpu.VMEM((height, 256), f32),
        ),
        in_specs=[SMEM] + [VMEM] * (3 + len(pieces)) + [ANY],
        out_specs=(VMEM, VMEM, VMEM),
        scratch_shapes=[
            pltpu.VMEM((count, LATENT + 2 * ROPE), bf16),
            pltpu.VMEM((2 * rows, count), f32),
        ],
        compiler_params=params(16),
        cost_estimate=cost(2 * height * count * (2 * LATENT + 2 * ROPE), height * count),
    )(starts, *held_in_vmem(q0, q1, wuk, *pieces, earlier))


def attention_second(starts, state, wuv, pieces, slots, half, earlier):
    heads = wuv.shape[1] // NOPE
    height = state[0].shape[0]
    rows = height // heads // 2
    count = 2 * rows * len(slots)
    wide = heads * NOPE
    return pl.pallas_call(
        functools.partial(second_kernel, rows, heads, half, slots),
        out_shape=(
            pltpu.VMEM((rows, wide), f32),
            pltpu.VMEM((rows, 128), f32),
            pltpu.VMEM((rows, wide + 128), bf16),
        ),
        in_specs=[SMEM] + [VMEM] * (4 + len(pieces)) + [ANY],
        out_specs=(VMEM, VMEM, VMEM),
        scratch_shapes=[
            pltpu.VMEM((count, LATENT + 2 * ROPE), bf16),
            pltpu.VMEM((2 * rows, count), f32),
        ],
        compiler_params=params(16),
        cost_estimate=cost(2 * height * count * (2 * LATENT + 2 * ROPE), height * count),
    )(starts, *held_in_vmem(*state, wuv, *pieces, earlier))


def combine_kernel(rows, heads, half, part, starts, lens, own, lse, got, *refs):
    out = refs[-1 - 2 * part]
    if part:
        weights, (copied, sem) = refs[-4], refs[-2:]
        moving = pltpu.make_async_copy(weights, copied, sem)
        moving.start()
    core = lax.axis_index("core")
    live = lens[core] - starts[core]
    base = lax.axis_index("yl") * half + lax.axis_index("z") * rows
    wide = heads * NOPE
    alive = base + lax.broadcasted_iota(jnp.int32, (rows, 1), 0) < live
    terms = got[:, wide : wide + 128].astype(f32)
    for h in range(heads):
        at = h * NOPE
        there = (
            terms[:, h : h + 1]
            + terms[:, heads + h : heads + h + 1]
            + terms[:, 2 * heads + h : 2 * heads + h + 1]
        )
        w = 1.0 / (1.0 + jnp.exp2(there - lse[:, h : h + 1]))
        o = own[:, at : at + NOPE] * w + got[:, at : at + NOPE].astype(f32) * (1.0 - w)
        at = part * wide + h * NOPE
        out[:, at : at + NOPE] = jnp.where(alive, o, 0.0).astype(bf16)
    if part:
        moving.wait()


def combine_first(starts, lens, own, lse, got, half, earlier):
    rows, wide = own.shape
    return pl.pallas_call(
        functools.partial(combine_kernel, rows, wide // NOPE, half, 0),
        out_shape=pltpu.VMEM((rows, 2 * wide), bf16),
        in_specs=[SMEM, SMEM] + [VMEM] * 3 + [ANY],
        out_specs=VMEM,
        compiler_params=params(2),
        cost_estimate=cost(8 * rows * wide),
    )(starts, lens, *held_in_vmem(own, lse, got, earlier))


def combine_second(starts, lens, own, lse, got, half, before, weights):
    rows, wide = own.shape
    return pl.pallas_call(
        functools.partial(combine_kernel, rows, wide // NOPE, half, 1),
        out_shape=(
            pltpu.VMEM((rows, 2 * wide), bf16),
            pltpu.VMEM(weights.shape, weights.dtype),
        ),
        in_specs=[SMEM, SMEM] + [VMEM] * 4 + [ANY],
        out_specs=(VMEM, ANY),
        scratch_shapes=[pltpu.SemaphoreType.DMA(())],
        input_output_aliases={5: 0},
        compiler_params=params(2),
        cost_estimate=cost(8 * rows * wide),
    )(starts, lens, *held_in_vmem(own, lse, got, before), weights)


NEAR = (0, 1, 2, 7, 6)
FAR = (3, 5, 4)


def products(pieces, weights, held):
    w00, w01, w10, w11 = weights
    depth = w00.shape[1]
    place = 0
    for piece in pieces:
        held[place : place + piece.shape[0], :] = piece[...]
        place += piece.shape[0]
    left = held[:, :depth]
    right = held[:, depth:]
    mine = nt(left, w00[...]) + nt(right, w10[...])
    other = nt(left, w01[...]) + nt(right, w11[...])
    swapped = lax.axis_index("yh") != lax.axis_index("yl")
    return jnp.concatenate(
        [jnp.where(swapped, other, mine), jnp.where(swapped, mine, other)], axis=1
    ).astype(bf16)


def near_kernel(*refs):
    count = len(NEAR)
    out, held = refs[-2:]
    out[...] = products(refs[:count], refs[count : count + 4], held)


def far_kernel(rows, *refs):
    near = refs[8]
    outs = refs[9:17]
    held, full = refs[17:]
    both = products(refs[:4], refs[4:8], held)
    for place, slot in enumerate(FAR):
        full[slot * rows : (slot + 1) * rows, :] = both[place * rows : (place + 1) * rows]
    for place, slot in enumerate(NEAR):
        full[slot * rows : (slot + 1) * rows, :] = near[place * rows : (place + 1) * rows, :]
    z, core, x = (lax.axis_index(name) for name in ("z", "core", "x"))
    odd = x & 1
    partners = (x, x + 1 - 2 * odd, (x - 1 + 2 * odd) & 3, (x + 2) & 3)
    for k, out in enumerate(outs):
        to_x, to_core = partners[k // 2], (core if k % 2 == 0 else 1 - core)
        slot = (z - 2 * to_x - to_core) & 7
        out[...] = full[pl.ds(pl.multiple_of(slot * rows, rows), rows), :]


def project_near(pieces, weights):
    rows, wide = pieces[0].shape
    cols = weights[0].shape[0]
    count = len(NEAR)
    return pl.pallas_call(
        near_kernel,
        out_shape=pltpu.VMEM((count * rows, 2 * cols), bf16),
        in_specs=[VMEM] * (count + 4),
        out_specs=VMEM,
        scratch_shapes=[pltpu.VMEM((count * rows, wide), bf16)],
        compiler_params=params(12),
        cost_estimate=cost(4 * count * rows * wide * cols),
    )(*held_in_vmem(*pieces, *weights))


def project_far(pieces, weights, near):
    rows, wide = pieces[0].shape
    cols = weights[0].shape[0]
    count = len(FAR)
    return pl.pallas_call(
        functools.partial(far_kernel, rows),
        out_shape=(pltpu.VMEM((rows, 2 * cols), bf16),) * 8,
        in_specs=[VMEM] * 9,
        out_specs=(VMEM,) * 8,
        scratch_shapes=[
            pltpu.VMEM((count * rows, wide), bf16),
            pltpu.VMEM((8 * rows, 2 * cols), bf16),
        ],
        compiler_params=params(12),
        cost_estimate=cost(4 * count * rows * wide * cols),
    )(*held_in_vmem(*pieces, *weights, near))


def level_kernel(*refs):
    pass


def level(arrays, earlier=()):
    count = len(arrays)
    return pl.pallas_call(
        level_kernel,
        out_shape=tuple(pltpu.VMEM(x.shape, x.dtype) for x in arrays),
        in_specs=[ANY] * (count + len(earlier)),
        out_specs=(ANY,) * count,
        input_output_aliases={i: i for i in range(count)},
        compiler_params=params(1),
    )(*held_in_vmem(*arrays, *earlier))


def swap(x, axis):
    return lax.ppermute(x, axis, [(0, 1), (1, 0)])


UP = [(i, (i + 1) % 8) for i in range(8)]
DOWN = [(i, (i - 1) % 8) for i in range(8)]


def step(a, b):
    return lax.ppermute(a, "z", UP), lax.ppermute(b, "z", DOWN)


def last(a, b):
    cut = a.shape[0] // 2
    return step(a[:cut], b[cut:])


X_PAIRS = ((1, 0, 3, 2), (3, 2, 1, 0), (2, 3, 0, 1))


def to_partner(x, pairs, flip):
    moves = [(2 * i + c, 2 * j + (c ^ flip)) for i, j in enumerate(pairs) for c in range(2)]
    return lax.ppermute(x, ("x", "core"), moves)


def pack_kernel(q_nope, q_rope, cache, stretch, latent, q_own, q_sent, sems):
    core = lax.axis_index("core")
    rows, wide = q_nope.shape[1:]
    moves = [
        (cache.at[core], latent.at[:rows, :]),
        (stretch.at[core], latent.at[rows:, :]),
        (q_nope.at[core], q_own.at[:, :wide]),
        (q_rope.at[core], q_own.at[:, wide:]),
        (q_nope.at[1 - core], q_sent.at[:, :wide]),
        (q_rope.at[1 - core], q_sent.at[:, wide:]),
    ]
    copies = [pltpu.make_async_copy(a, b, sems.at[i]) for i, (a, b) in enumerate(moves)]
    for copy in copies:
        copy.start()
    for copy in copies:
        copy.wait()


def pack(q_nope, q_rope, cache, stretch):
    rows, width = cache.shape[1:]
    wide = q_nope.shape[2] + q_rope.shape[2]
    return pl.pallas_call(
        pack_kernel,
        out_shape=(
            pltpu.VMEM((2 * rows, width), bf16),
            pltpu.VMEM((rows, wide), bf16),
            pltpu.VMEM((rows, wide), bf16),
        ),
        in_specs=[ANY] * 4,
        out_specs=(ANY,) * 3,
        scratch_shapes=[pltpu.SemaphoreType.DMA((6,))],
        compiler_params=params(1),
    )(*in_hbm(q_nope, q_rope, cache, stretch))


def sum_kernel(*refs):
    parts, (first, second) = refs[:8], refs[8:]
    core = lax.axis_index("core")
    cols = first.shape[2]
    for k in range(2):
        total = parts[4 * k][...].astype(f32)
        for part in parts[4 * k + 1 : 4 * k + 4]:
            total += part[...].astype(f32)
        total = total.astype(bf16)
        to = core if k == 0 else 1 - core
        first[to] = total[:, :cols]
        second[to] = total[:, cols:]


def sums(own_seq, other_seq):
    rows, cols = own_seq[0].shape
    out = pltpu.VMEM((2, rows, cols // 2), bf16)
    return pl.pallas_call(
        sum_kernel,
        out_shape=(out, out),
        in_specs=[VMEM] * 8,
        out_specs=(VMEM, VMEM),
        compiler_params=params(4),
    )(*held_in_vmem(*own_seq, *other_seq))


def local(q_nope, q_rope, cache_latent, stretch_latent, w_uk, w_uv, w_o, stretch_start, prompt_len):
    half = 8 * q_nope.shape[1]
    latent, q_own, q_sent = pack(q_nope, q_rope, cache_latent, stretch_latent)
    q_own_y = swap(q_own, "yl")
    q_got = swap(q_sent, "core")
    u1, d1, q_got = level((*step(latent, latent), q_got))
    u2, d2, q_got = level((*step(u1, d1), q_got))
    q_got_y = swap(q_got, "yl")
    w_uk2 = swap(w_uk, "core")
    w_uv2 = swap(w_uv, "core")
    near = [latent, u1, u2, d1]
    near_at, far_at = (0, 1, 2, 7), (6, 3, 5, 4)
    a1 = attention_first(stretch_start, q_own, q_own_y, w_uk, near, near_at, half, u1)
    u3, d3 = level(step(u2, d2), (q_got_y, w_uk2, w_uv2, a1[2]))
    b1 = attention_first(stretch_start, q_got, q_got_y, w_uk2, near, near_at, half, u3)
    far = [d2, u3, d3, *last(u3, d3)]
    a2 = attention_second(stretch_start, a1, w_uv, far, far_at, half, b1[2])
    got_a = swap(a2[2], "yl")
    b2 = attention_second(stretch_start, b1, w_uv2, far, far_at, half, a2[1])
    got_b = swap(b2[2], "yl")
    known = (stretch_start, prompt_len)
    attention = combine_first(*known, *a2[:2], got_a, half, b2[1])
    attention, w_t = combine_second(*known, *b2[:2], got_b, half, attention, w_o.T)

    u1, d1 = level(step(attention, attention))
    w_t_c = swap(w_t, "core")
    w_t_y = swap(w_t, "yl")
    u2, d2 = level(step(u1, d1), (w_t_c,))
    u3, d3, w_t_y = level((*step(u2, d2), w_t_y))
    w_t_cy = swap(w_t_y, "core")
    weights = (w_t, w_t_y, w_t_c, w_t_cy)
    near = project_near([attention, u1, u2, d1, d2], weights)
    parts = project_far([u3, d3, *last(u3, d3)], weights, near)

    other_seq = [swap(parts[1], "core")]
    other_seq += [to_partner(parts[2 * k + 3], X_PAIRS[k], 1) for k in range(3)]
    own_seq = [parts[0]] + [to_partner(parts[2 * k + 2], X_PAIRS[k], 0) for k in range(3)]
    first, second = sums(own_seq, other_seq)
    first = lax.ppermute(first, ("yl", "yh"), [(0, 0), (1, 2), (2, 1), (3, 3)])
    second = lax.ppermute(second, ("yl", "yh"), [(0, 2), (2, 3), (1, 0), (3, 1)])
    return (first.astype(f32) + second.astype(f32)).astype(bf16)


def solution(mesh):
    fine = Mesh(mesh.devices.reshape(2, 8, 2, 4, 2), ("yl", "z", "yh", "x", "core"))
    ctx = ("yl", "z")
    head = ("yh", "x", "core")
    placed = (
        P(None, ctx, head),
        P(None, ctx, head),
        P(None, ctx, None),
        P(None, ctx, None),
        P(None, head),
        P(None, head),
        P(head, ctx),
        P(),
        P(),
    )
    return jax.shard_map(
        local, mesh=fine, in_specs=placed, out_specs=P(None, head, ctx), check_vma=False
    )
```

```python
import functools

import jax
import jax.numpy as jnp
from jax import lax
from jax.experimental import pallas as pl
from jax.experimental.pallas import tpu as pltpu
from jax.sharding import Mesh, PartitionSpec as P

LATENT = 512
ROPE = 64
NOPE = 128
LOG2E = 1.4426950408889634
HIDDEN = -1e30
GROUP = 8
MIB = 1024 * 1024

f32 = jnp.float32
bf16 = jnp.bfloat16


def nt(a, b):
    return lax.dot_general(a, b, (((1,), (1,)), ((), ())), preferred_element_type=f32)


def nn(a, b):
    return jnp.dot(a, b, preferred_element_type=f32)


def load_keys(rows, slots, pieces, keys):
    place = 0
    for piece in pieces:
        height = piece.shape[0]
        value = piece[...]
        keys[place : place + height, :LATENT] = value[:, :LATENT]
        rope = value[:, LATENT:]
        keys[place : place + height, LATENT:] = jnp.concatenate([rope, rope], axis=1)
        place += height


def hidden_keys(rows, slots, half, starts):
    y, z = lax.axis_index("yl"), lax.axis_index("z")
    start = starts[lax.axis_index("core")]
    row = lax.broadcasted_iota(jnp.int32, (2 * rows, 2 * rows), 0)
    col = lax.broadcasted_iota(jnp.int32, (2 * rows, 2 * rows), 1)
    partner = (row >= rows).astype(jnp.int32)
    q_y = y + partner * (1 - 2 * y)
    q_pos = q_y * half + z * rows + row - partner * rows
    in_cache = col < rows
    limit = jnp.where(in_cache, start, q_pos + 1)
    inner = y * half + jnp.where(in_cache, col, col - rows)
    return jnp.concatenate(
        [
            jnp.where(inner + ((z - d) & 7) * rows < limit, 0.0, HIDDEN).astype(f32)
            for d in slots
        ],
        axis=1,
    )


def scores_of(q, keys, bias):
    s = nt(q, keys[...])
    height, count = bias.shape
    return (s.reshape(GROUP, height, count) + bias[...][None]).reshape(GROUP * height, count)


def tiled(x, like):
    return jnp.concatenate([x] * (like.shape[1] // 128), axis=1)


def first_kernel(rows, heads, half, slots, *refs):
    c = (NOPE + ROPE) ** -0.5 * LOG2E
    starts, q0, q1, wuk = refs[:4]
    pieces = refs[4 : 4 + len(slots)]
    rest = refs[5 + len(slots) :]
    moving = None
    if len(rest) > 5:
        moving = pltpu.make_async_copy(rest[0], rest[4], rest[-1])
        moving.start()
        rest = (*rest[1:4], *rest[5:7])
    qaug, acc, stats, keys, bias = rest
    load_keys(rows, slots, pieces, keys)
    bias[...] = hidden_keys(rows, slots, half, starts)
    wide = heads * NOPE
    block = GROUP * 2 * rows
    low = lax.broadcasted_iota(jnp.int32, (2 * rows, 2 * ROPE), 1) < ROPE
    for g in range(heads // GROUP):
        for j in range(GROUP):
            h = g * GROUP + j
            at = h * NOPE
            q = jnp.concatenate([q0[:, at : at + NOPE], q1[:, at : at + NOPE]], axis=0)
            r0 = wide + (h // 2) * 2 * ROPE
            r = jnp.concatenate([q0[:, r0 : r0 + 2 * ROPE], q1[:, r0 : r0 + 2 * ROPE]], axis=0)
            keep = low if h % 2 == 0 else jnp.logical_not(low)
            base = h * 2 * rows
            qaug[base : base + 2 * rows, :LATENT] = nt(q, wuk[:, at : at + NOPE]).astype(bf16)
            qaug[base : base + 2 * rows, LATENT:] = jnp.where(keep, r, jnp.zeros_like(r))
        here = slice(g * block, (g + 1) * block)
        s = scores_of(qaug[here], keys, bias)
        m = jnp.broadcast_to(jnp.max(s, axis=-1, keepdims=True), (block, 128))
        p = jnp.exp2((s - tiled(m, s)) * c)
        acc[here] = nn(p.astype(bf16), keys[:, :LATENT])
        stats[here, :128] = m
        stats[here, 128:] = jnp.broadcast_to(jnp.sum(p, axis=-1, keepdims=True), (block, 128))
    if moving is not None:
        moving.wait()


def second_kernel(rows, heads, half, slots, *refs):
    c = (NOPE + ROPE) ** -0.5 * LOG2E
    starts, qaug, acc, stats, wuv = refs[:5]
    pieces = refs[5 : 6 + len(slots)]
    own, own_lse, message, keys, bias = refs[-5:]
    load_keys(rows, slots, pieces, keys)
    bias[...] = hidden_keys(rows, slots, half, starts)
    wide = heads * NOPE
    block = GROUP * 2 * rows
    out_lane = lax.broadcasted_iota(jnp.int32, (rows, 128), 1)
    own_all = jnp.zeros((rows, 128), f32)
    sent_all = jnp.zeros((rows, 128), f32)
    for g in range(heads // GROUP):
        here = slice(g * block, (g + 1) * block)
        s = scores_of(qaug[here], keys, bias)
        m1 = stats[here, :128]
        m = jnp.maximum(m1, jnp.max(s, axis=-1, keepdims=True))
        factor = jnp.exp2((m1 - m) * c)
        p = jnp.exp2((s - tiled(m, s)) * c)
        total = stats[here, 128:] * factor + jnp.sum(p, axis=-1, keepdims=True)
        fresh = nn(p.astype(bf16), keys[:, :LATENT])
        inverse = 1.0 / total
        mixed = acc[here] * tiled(factor * inverse, fresh) + fresh * tiled(inverse, fresh)
        mixed = mixed.astype(bf16)
        lse = m * c + jnp.log2(total)
        for j in range(GROUP):
            h = g * GROUP + j
            at = h * NOPE
            base = j * 2 * rows
            o = nn(mixed[base : base + 2 * rows], wuv[:, at : at + NOPE])
            own[:, at : at + NOPE] = o[:rows]
            message[:, at : at + NOPE] = o[rows:].astype(bf16)
            own_all = jnp.where(out_lane == h, lse[base : base + rows], own_all)
            rest = lse[base + rows : base + 2 * rows]
            for term in range(3):
                part = rest.astype(bf16).astype(f32)
                sent_all = jnp.where(out_lane == term * heads + h, part, sent_all)
                rest = rest - part
    own_lse[...] = own_all
    message[:, wide : wide + 128] = sent_all.astype(bf16)


VMEM = pl.BlockSpec(memory_space=pltpu.VMEM)
SMEM = pl.BlockSpec(memory_space=pltpu.SMEM)
ANY = pl.BlockSpec(memory_space=pl.ANY)


def params(mib):
    return pltpu.CompilerParams(vmem_limit_bytes=mib * MIB)


def held_in_vmem(*arrays):
    return tuple(pltpu.with_memory_space_constraint(x, pltpu.VMEM) for x in arrays)


def in_hbm(*arrays):
    return tuple(pltpu.with_memory_space_constraint(x, pltpu.HBM) for x in arrays)


def cost(flops, exps=0):
    return pl.CostEstimate(flops=flops, transcendentals=exps, bytes_accessed=4 * MIB)


def attention_first(starts, q0, q1, wuk, pieces, slots, half, earlier, weights=None):
    rows = q0.shape[0]
    heads = wuk.shape[1] // NOPE
    height = heads * 2 * rows
    count = 2 * rows * len(slots)
    carried = () if weights is None else in_hbm(weights)
    return pl.pallas_call(
        functools.partial(first_kernel, rows, heads, half, slots),
        out_shape=(
            pltpu.VMEM((height, LATENT + 2 * ROPE), bf16),
            pltpu.VMEM((height, LATENT), f32),
            pltpu.VMEM((height, 256), f32),
            *(pltpu.VMEM(x.shape, bf16) for x in carried),
        ),
        in_specs=[SMEM] + [VMEM] * (3 + len(pieces)) + [ANY] * (1 + len(carried)),
        out_specs=(VMEM,) * 3 + (ANY,) * len(carried),
        scratch_shapes=[
            pltpu.VMEM((count, LATENT + 2 * ROPE), bf16),
            pltpu.VMEM((2 * rows, count), f32),
        ]
        + [pltpu.SemaphoreType.DMA(())] * len(carried),
        compiler_params=params(16),
        cost_estimate=cost(2 * height * count * (2 * LATENT + 2 * ROPE), height * count),
    )(starts, *held_in_vmem(q0, q1, wuk, *pieces, earlier), *carried)


def attention_second(starts, state, wuv, pieces, slots, half, *earlier):
    heads = wuv.shape[1] // NOPE
    height = state[0].shape[0]
    rows = height // heads // 2
    count = 2 * rows * len(slots)
    wide = heads * NOPE
    return pl.pallas_call(
        functools.partial(second_kernel, rows, heads, half, slots),
        out_shape=(
            pltpu.VMEM((rows, wide), f32),
            pltpu.VMEM((rows, 128), f32),
            pltpu.VMEM((rows, wide + 128), bf16),
        ),
        in_specs=[SMEM] + [VMEM] * (4 + len(pieces)) + [ANY] * len(earlier),
        out_specs=(VMEM, VMEM, VMEM),
        scratch_shapes=[
            pltpu.VMEM((count, LATENT + 2 * ROPE), bf16),
            pltpu.VMEM((2 * rows, count), f32),
        ],
        compiler_params=params(16),
        cost_estimate=cost(2 * height * count * (2 * LATENT + 2 * ROPE), height * count),
    )(starts, *held_in_vmem(*state, wuv, *pieces, *earlier))


def combine_kernel(rows, heads, half, part, starts, lens, own, lse, got, *refs):
    out = refs[-1 - 2 * part]
    if part:
        weights, (copied, sem) = refs[-4], refs[-2:]
        moving = pltpu.make_async_copy(weights, copied, sem)
        moving.start()
    core = lax.axis_index("core")
    live = lens[core] - starts[core]
    base = lax.axis_index("yl") * half + lax.axis_index("z") * rows
    wide = heads * NOPE
    alive = base + lax.broadcasted_iota(jnp.int32, (rows, 1), 0) < live
    terms = got[:, wide : wide + 128].astype(f32)
    for h in range(heads):
        at = h * NOPE
        there = (
            terms[:, h : h + 1]
            + terms[:, heads + h : heads + h + 1]
            + terms[:, 2 * heads + h : 2 * heads + h + 1]
        )
        w = 1.0 / (1.0 + jnp.exp2(there - lse[:, h : h + 1]))
        o = own[:, at : at + NOPE] * w + got[:, at : at + NOPE].astype(f32) * (1.0 - w)
        at = part * wide + h * NOPE
        out[:, at : at + NOPE] = jnp.where(alive, o, 0.0).astype(bf16)
    if part:
        moving.wait()


def combine_first(starts, lens, own, lse, got, half, earlier):
    rows, wide = own.shape
    return pl.pallas_call(
        functools.partial(combine_kernel, rows, wide // NOPE, half, 0),
        out_shape=pltpu.VMEM((rows, 2 * wide), bf16),
        in_specs=[SMEM, SMEM] + [VMEM] * 3 + [ANY],
        out_specs=VMEM,
        compiler_params=params(2),
        cost_estimate=cost(8 * rows * wide),
    )(starts, lens, *held_in_vmem(own, lse, got, earlier))


def combine_second(starts, lens, own, lse, got, half, before, weights):
    rows, wide = own.shape
    return pl.pallas_call(
        functools.partial(combine_kernel, rows, wide // NOPE, half, 1),
        out_shape=(
            pltpu.VMEM((rows, 2 * wide), bf16),
            pltpu.VMEM(weights.shape, weights.dtype),
        ),
        in_specs=[SMEM, SMEM] + [VMEM] * 4 + [ANY],
        out_specs=(VMEM, ANY),
        scratch_shapes=[pltpu.SemaphoreType.DMA(())],
        input_output_aliases={5: 0},
        compiler_params=params(2),
        cost_estimate=cost(8 * rows * wide),
    )(starts, lens, *held_in_vmem(own, lse, got, before), weights)


NEAR = (0, 1, 2, 7, 6)
FAR = (3, 5, 4)


def products(pieces, weights, held):
    w00, w01, w10, w11 = weights
    depth = w00.shape[1]
    place = 0
    for piece in pieces:
        held[place : place + piece.shape[0], :] = piece[...]
        place += piece.shape[0]
    left = held[:, :depth]
    right = held[:, depth:]
    mine = nt(left, w00[...]) + nt(right, w10[...])
    other = nt(left, w01[...]) + nt(right, w11[...])
    swapped = lax.axis_index("yh") != lax.axis_index("yl")
    return jnp.concatenate(
        [jnp.where(swapped, other, mine), jnp.where(swapped, mine, other)], axis=1
    ).astype(bf16)


def near_kernel(*refs):
    count = len(NEAR)
    out, held = refs[-2:]
    out[...] = products(refs[:count], refs[count : count + 4], held)


def far_kernel(rows, *refs):
    near = refs[8]
    outs = refs[9:17]
    held, full = refs[17:]
    both = products(refs[:4], refs[4:8], held)
    for place, slot in enumerate(FAR):
        full[slot * rows : (slot + 1) * rows, :] = both[place * rows : (place + 1) * rows]
    for place, slot in enumerate(NEAR):
        full[slot * rows : (slot + 1) * rows, :] = near[place * rows : (place + 1) * rows, :]
    z, core, x = (lax.axis_index(name) for name in ("z", "core", "x"))
    odd = x & 1
    partners = (x, x + 1 - 2 * odd, (x - 1 + 2 * odd) & 3, (x + 2) & 3)
    for k, out in enumerate(outs):
        to_x, to_core = partners[k // 2], (core if k % 2 == 0 else 1 - core)
        slot = (z - 2 * to_x - to_core) & 7
        out[...] = full[pl.ds(pl.multiple_of(slot * rows, rows), rows), :]


def project_near(pieces, weights):
    rows, wide = pieces[0].shape
    cols = weights[0].shape[0]
    count = len(NEAR)
    return pl.pallas_call(
        near_kernel,
        out_shape=pltpu.VMEM((count * rows, 2 * cols), bf16),
        in_specs=[VMEM] * (count + 4),
        out_specs=VMEM,
        scratch_shapes=[pltpu.VMEM((count * rows, wide), bf16)],
        compiler_params=params(12),
        cost_estimate=cost(4 * count * rows * wide * cols),
    )(*held_in_vmem(*pieces, *weights))


def project_far(pieces, weights, near):
    rows, wide = pieces[0].shape
    cols = weights[0].shape[0]
    count = len(FAR)
    return pl.pallas_call(
        functools.partial(far_kernel, rows),
        out_shape=(pltpu.VMEM((rows, 2 * cols), bf16),) * 8,
        in_specs=[VMEM] * 9,
        out_specs=(VMEM,) * 8,
        scratch_shapes=[
            pltpu.VMEM((count * rows, wide), bf16),
            pltpu.VMEM((8 * rows, 2 * cols), bf16),
        ],
        compiler_params=params(12),
        cost_estimate=cost(4 * count * rows * wide * cols),
    )(*held_in_vmem(*pieces, *weights, near))


def level_kernel(*refs):
    pass


def level(arrays, earlier=()):
    count = len(arrays)
    return pl.pallas_call(
        level_kernel,
        out_shape=tuple(pltpu.VMEM(x.shape, x.dtype) for x in arrays),
        in_specs=[ANY] * (count + len(earlier)),
        out_specs=(ANY,) * count,
        input_output_aliases={i: i for i in range(count)},
        compiler_params=params(1),
    )(*held_in_vmem(*arrays, *earlier))


def swap(x, axis):
    return lax.ppermute(x, axis, [(0, 1), (1, 0)])


UP = [(i, (i + 1) % 8) for i in range(8)]
DOWN = [(i, (i - 1) % 8) for i in range(8)]


def step(a, b):
    return lax.ppermute(a, "z", UP), lax.ppermute(b, "z", DOWN)


def last(a, b):
    cut = a.shape[0] // 2
    return step(a[:cut], b[cut:])


X_PAIRS = ((1, 0, 3, 2), (3, 2, 1, 0), (2, 3, 0, 1))


def to_partner(x, pairs, flip):
    moves = [(2 * i + c, 2 * j + (c ^ flip)) for i, j in enumerate(pairs) for c in range(2)]
    return lax.ppermute(x, ("x", "core"), moves)


def pack_kernel(q_nope, q_rope, cache, stretch, latent, q_own, q_sent, sems):
    core = lax.axis_index("core")
    rows, wide = q_nope.shape[1:]
    moves = [
        (cache.at[core], latent.at[:rows, :]),
        (stretch.at[core], latent.at[rows:, :]),
        (q_nope.at[core], q_own.at[:, :wide]),
        (q_rope.at[core], q_own.at[:, wide:]),
        (q_nope.at[1 - core], q_sent.at[:, :wide]),
        (q_rope.at[1 - core], q_sent.at[:, wide:]),
    ]
    copies = [pltpu.make_async_copy(a, b, sems.at[i]) for i, (a, b) in enumerate(moves)]
    for copy in copies:
        copy.start()
    for copy in copies:
        copy.wait()


def pack(q_nope, q_rope, cache, stretch):
    rows, width = cache.shape[1:]
    wide = q_nope.shape[2] + q_rope.shape[2]
    return pl.pallas_call(
        pack_kernel,
        out_shape=(
            pltpu.VMEM((2 * rows, width), bf16),
            pltpu.VMEM((rows, wide), bf16),
            pltpu.VMEM((rows, wide), bf16),
        ),
        in_specs=[ANY] * 4,
        out_specs=(ANY,) * 3,
        scratch_shapes=[pltpu.SemaphoreType.DMA((6,))],
        compiler_params=params(1),
    )(*in_hbm(q_nope, q_rope, cache, stretch))


def sum_kernel(*refs):
    parts, (first, second) = refs[:8], refs[8:]
    core = lax.axis_index("core")
    cols = first.shape[2]
    for k in range(2):
        total = parts[4 * k][...].astype(f32)
        for part in parts[4 * k + 1 : 4 * k + 4]:
            total += part[...].astype(f32)
        total = total.astype(bf16)
        to = core if k == 0 else 1 - core
        first[to] = total[:, :cols]
        second[to] = total[:, cols:]


def sums(own_seq, other_seq):
    rows, cols = own_seq[0].shape
    out = pltpu.VMEM((2, rows, cols // 2), bf16)
    return pl.pallas_call(
        sum_kernel,
        out_shape=(out, out),
        in_specs=[VMEM] * 8,
        out_specs=(VMEM, VMEM),
        compiler_params=params(4),
    )(*held_in_vmem(*own_seq, *other_seq))


def local(q_nope, q_rope, cache_latent, stretch_latent, w_uk, w_uv, w_o, stretch_start, prompt_len):
    half = 8 * q_nope.shape[1]
    latent, q_own, q_sent = pack(q_nope, q_rope, cache_latent, stretch_latent)
    q_own_y = swap(q_own, "yl")
    q_got = swap(q_sent, "core")
    u1, d1, q_got = level((*step(latent, latent), q_got))
    u2, d2, q_got = level((*step(u1, d1), q_got))
    q_got_y = swap(q_got, "yl")
    w_uk2 = swap(w_uk, "core")
    w_uv2 = swap(w_uv, "core")
    near = [latent, u1, u2, d1]
    near_at, far_at = (0, 1, 2, 7), (6, 3, 5, 4)
    *a1, w_t = attention_first(
        stretch_start, q_own, q_own_y, w_uk, near, near_at, half, u1, w_o.T
    )
    u3, d3, w_t = level((*step(u2, d2), w_t), (q_got_y, w_uk2, w_uv2, a1[2]))
    w_t_c = swap(w_t, "core")
    b1 = attention_first(stretch_start, q_got, q_got_y, w_uk2, near, near_at, half, u3)
    far = [d2, u3, d3, *last(u3, d3)]
    a2 = attention_second(stretch_start, a1, w_uv, far, far_at, half, b1[2])
    got_a = swap(a2[2], "yl")
    b2 = attention_second(stretch_start, b1, w_uv2, far, far_at, half, a2[1], w_t_c)
    got_b = swap(b2[2], "yl")
    known = (stretch_start, prompt_len)
    attention = combine_first(*known, *a2[:2], got_a, half, b2[1])
    attention, w_t = combine_second(*known, *b2[:2], got_b, half, attention, w_o.T)

    u1, d1 = level(step(attention, attention))
    w_t_y = swap(w_t, "yl")
    u2, d2 = level(step(u1, d1))
    u3, d3, w_t_y = level((*step(u2, d2), w_t_y))
    w_t_cy = swap(w_t_y, "core")
    weights = (w_t, w_t_y, w_t_c, w_t_cy)
    near = project_near([attention, u1, u2, d1, d2], weights)
    parts = project_far([u3, d3, *last(u3, d3)], weights, near)

    other_seq = [swap(parts[1], "core")]
    other_seq += [to_partner(parts[2 * k + 3], X_PAIRS[k], 1) for k in range(3)]
    own_seq = [parts[0]] + [to_partner(parts[2 * k + 2], X_PAIRS[k], 0) for k in range(3)]
    first, second = sums(own_seq, other_seq)
    first = lax.ppermute(first, ("yl", "yh"), [(0, 0), (1, 2), (2, 1), (3, 3)])
    second = lax.ppermute(second, ("yl", "yh"), [(0, 2), (2, 3), (1, 0), (3, 1)])
    return (first.astype(f32) + second.astype(f32)).astype(bf16)


def solution(mesh):
    fine = Mesh(mesh.devices.reshape(2, 8, 2, 4, 2), ("yl", "z", "yh", "x", "core"))
    ctx = ("yl", "z")
    head = ("yh", "x", "core")
    placed = (
        P(None, ctx, head),
        P(None, ctx, head),
        P(None, ctx, None),
        P(None, ctx, None),
        P(None, head),
        P(None, head),
        P(head, ctx),
        P(),
        P(),
    )
    return jax.shard_map(
        local, mesh=fine, in_specs=placed, out_specs=P(None, head, ctx), check_vma=False
    )
```

```python
import functools

import jax
import jax.numpy as jnp
from jax import lax
from jax.experimental import pallas as pl
from jax.experimental.pallas import tpu as pltpu
from jax.sharding import Mesh, PartitionSpec as P

LATENT = 512
ROPE = 64
NOPE = 128
LOG2E = 1.4426950408889634
HIDDEN = -1e30
GROUP = 8
MIB = 1024 * 1024

f32 = jnp.float32
bf16 = jnp.bfloat16


def nt(a, b):
    return lax.dot_general(a, b, (((1,), (1,)), ((), ())), preferred_element_type=f32)


def nn(a, b):
    return jnp.dot(a, b, preferred_element_type=f32)


def load_keys(rows, slots, pieces, keys):
    place = 0
    for piece in pieces:
        height = piece.shape[0]
        value = piece[...]
        keys[place : place + height, :LATENT] = value[:, :LATENT]
        rope = value[:, LATENT:]
        keys[place : place + height, LATENT:] = jnp.concatenate([rope, rope], axis=1)
        place += height


def hidden_keys(rows, slots, half, starts):
    y, z = lax.axis_index("yl"), lax.axis_index("z")
    start = starts[lax.axis_index("core")]
    row = lax.broadcasted_iota(jnp.int32, (2 * rows, 2 * rows), 0)
    col = lax.broadcasted_iota(jnp.int32, (2 * rows, 2 * rows), 1)
    partner = (row >= rows).astype(jnp.int32)
    q_y = y + partner * (1 - 2 * y)
    q_pos = q_y * half + z * rows + row - partner * rows
    in_cache = col < rows
    limit = jnp.where(in_cache, start, q_pos + 1)
    inner = y * half + jnp.where(in_cache, col, col - rows)
    return jnp.concatenate(
        [
            jnp.where(inner + ((z - d) & 7) * rows < limit, 0.0, HIDDEN).astype(f32)
            for d in slots
        ],
        axis=1,
    )


def scores_of(q, keys, bias):
    s = nt(q, keys[...])
    height, count = bias.shape
    return (s.reshape(GROUP, height, count) + bias[...][None]).reshape(GROUP * height, count)


def tiled(x, like):
    return jnp.concatenate([x] * (like.shape[1] // 128), axis=1)


def first_kernel(rows, heads, half, slots, *refs):
    c = (NOPE + ROPE) ** -0.5 * LOG2E
    starts, q0, q1, wuk = refs[:4]
    pieces = refs[4 : 4 + len(slots)]
    rest = refs[5 + len(slots) :]
    moving = None
    if len(rest) > 5:
        moving = pltpu.make_async_copy(rest[0], rest[4], rest[-1])
        moving.start()
        rest = (*rest[1:4], *rest[5:7])
    qaug, acc, stats, keys, bias = rest
    load_keys(rows, slots, pieces, keys)
    bias[...] = hidden_keys(rows, slots, half, starts)
    wide = heads * NOPE
    block = GROUP * 2 * rows
    low = lax.broadcasted_iota(jnp.int32, (2 * rows, 2 * ROPE), 1) < ROPE
    for g in range(heads // GROUP):
        for j in range(GROUP):
            h = g * GROUP + j
            at = h * NOPE
            q = jnp.concatenate([q0[:, at : at + NOPE], q1[:, at : at + NOPE]], axis=0)
            r0 = wide + (h // 2) * 2 * ROPE
            r = jnp.concatenate([q0[:, r0 : r0 + 2 * ROPE], q1[:, r0 : r0 + 2 * ROPE]], axis=0)
            keep = low if h % 2 == 0 else jnp.logical_not(low)
            base = h * 2 * rows
            qaug[base : base + 2 * rows, :LATENT] = nt(q, wuk[:, at : at + NOPE]).astype(bf16)
            qaug[base : base + 2 * rows, LATENT:] = jnp.where(keep, r, jnp.zeros_like(r))
        here = slice(g * block, (g + 1) * block)
        s = scores_of(qaug[here], keys, bias)
        m = jnp.broadcast_to(jnp.max(s, axis=-1, keepdims=True), (block, 128))
        p = jnp.exp2((s - tiled(m, s)) * c)
        acc[here] = nn(p.astype(bf16), keys[:, :LATENT])
        stats[here, :128] = m
        stats[here, 128:] = jnp.broadcast_to(jnp.sum(p, axis=-1, keepdims=True), (block, 128))
    if moving is not None:
        moving.wait()


def second_kernel(rows, heads, half, slots, *refs):
    c = (NOPE + ROPE) ** -0.5 * LOG2E
    starts, qaug, acc, stats, wuv = refs[:5]
    pieces = refs[5 : 6 + len(slots)]
    own, own_lse, message, keys, bias = refs[-5:]
    load_keys(rows, slots, pieces, keys)
    bias[...] = hidden_keys(rows, slots, half, starts)
    wide = heads * NOPE
    block = GROUP * 2 * rows
    out_lane = lax.broadcasted_iota(jnp.int32, (rows, 128), 1)
    own_all = jnp.zeros((rows, 128), f32)
    sent_all = jnp.zeros((rows, 128), f32)
    for g in range(heads // GROUP):
        here = slice(g * block, (g + 1) * block)
        s = scores_of(qaug[here], keys, bias)
        m1 = stats[here, :128]
        m = jnp.maximum(m1, jnp.max(s, axis=-1, keepdims=True))
        factor = jnp.exp2((m1 - m) * c)
        p = jnp.exp2((s - tiled(m, s)) * c)
        total = stats[here, 128:] * factor + jnp.sum(p, axis=-1, keepdims=True)
        fresh = nn(p.astype(bf16), keys[:, :LATENT])
        inverse = 1.0 / total
        mixed = acc[here] * tiled(factor * inverse, fresh) + fresh * tiled(inverse, fresh)
        mixed = mixed.astype(bf16)
        lse = m * c + jnp.log2(total)
        for j in range(GROUP):
            h = g * GROUP + j
            at = h * NOPE
            base = j * 2 * rows
            o = nn(mixed[base : base + 2 * rows], wuv[:, at : at + NOPE])
            own[:, at : at + NOPE] = o[:rows]
            message[:, at : at + NOPE] = o[rows:].astype(bf16)
            own_all = jnp.where(out_lane == h, lse[base : base + rows], own_all)
            rest = lse[base + rows : base + 2 * rows]
            for term in range(3):
                part = rest.astype(bf16).astype(f32)
                sent_all = jnp.where(out_lane == term * heads + h, part, sent_all)
                rest = rest - part
    own_lse[...] = own_all
    message[:, wide : wide + 128] = sent_all.astype(bf16)


VMEM = pl.BlockSpec(memory_space=pltpu.VMEM)
SMEM = pl.BlockSpec(memory_space=pltpu.SMEM)
ANY = pl.BlockSpec(memory_space=pl.ANY)


def params(mib):
    return pltpu.CompilerParams(vmem_limit_bytes=mib * MIB)


def held_in_vmem(*arrays):
    return tuple(pltpu.with_memory_space_constraint(x, pltpu.VMEM) for x in arrays)


def in_hbm(*arrays):
    return tuple(pltpu.with_memory_space_constraint(x, pltpu.HBM) for x in arrays)


def cost(flops, exps=0):
    return pl.CostEstimate(flops=flops, transcendentals=exps, bytes_accessed=4 * MIB)


def attention_first(starts, q0, q1, wuk, pieces, slots, half, earlier, weights=None):
    rows = q0.shape[0]
    heads = wuk.shape[1] // NOPE
    height = heads * 2 * rows
    count = 2 * rows * len(slots)
    carried = () if weights is None else in_hbm(weights)
    return pl.pallas_call(
        functools.partial(first_kernel, rows, heads, half, slots),
        out_shape=(
            pltpu.VMEM((height, LATENT + 2 * ROPE), bf16),
            pltpu.VMEM((height, LATENT), f32),
            pltpu.VMEM((height, 256), f32),
            *(pltpu.VMEM(x.shape, bf16) for x in carried),
        ),
        in_specs=[SMEM] + [VMEM] * (3 + len(pieces)) + [ANY] * (1 + len(carried)),
        out_specs=(VMEM,) * 3 + (ANY,) * len(carried),
        scratch_shapes=[
            pltpu.VMEM((count, LATENT + 2 * ROPE), bf16),
            pltpu.VMEM((2 * rows, count), f32),
        ]
        + [pltpu.SemaphoreType.DMA(())] * len(carried),
        compiler_params=params(16),
        cost_estimate=cost(2 * height * count * (2 * LATENT + 2 * ROPE), height * count),
    )(starts, *held_in_vmem(q0, q1, wuk, *pieces, earlier), *carried)


def attention_second(starts, state, wuv, pieces, slots, half, *earlier):
    heads = wuv.shape[1] // NOPE
    height = state[0].shape[0]
    rows = height // heads // 2
    count = 2 * rows * len(slots)
    wide = heads * NOPE
    return pl.pallas_call(
        functools.partial(second_kernel, rows, heads, half, slots),
        out_shape=(
            pltpu.VMEM((rows, wide), f32),
            pltpu.VMEM((rows, 128), f32),
            pltpu.VMEM((rows, wide + 128), bf16),
        ),
        in_specs=[SMEM] + [VMEM] * (4 + len(pieces)) + [ANY] * len(earlier),
        out_specs=(VMEM, VMEM, VMEM),
        scratch_shapes=[
            pltpu.VMEM((count, LATENT + 2 * ROPE), bf16),
            pltpu.VMEM((2 * rows, count), f32),
        ],
        compiler_params=params(16),
        cost_estimate=cost(2 * height * count * (2 * LATENT + 2 * ROPE), height * count),
    )(starts, *held_in_vmem(*state, wuv, *pieces, *earlier))


def combine_kernel(rows, heads, half, part, starts, lens, own, lse, got, *refs):
    out = refs[-1 - 2 * part]
    if part:
        weights, (copied, sem) = refs[-4], refs[-2:]
        moving = pltpu.make_async_copy(weights, copied, sem)
        moving.start()
    core = lax.axis_index("core")
    live = lens[core] - starts[core]
    base = lax.axis_index("yl") * half + lax.axis_index("z") * rows
    wide = heads * NOPE
    alive = base + lax.broadcasted_iota(jnp.int32, (rows, 1), 0) < live
    terms = got[:, wide : wide + 128].astype(f32)
    for h in range(heads):
        at = h * NOPE
        there = (
            terms[:, h : h + 1]
            + terms[:, heads + h : heads + h + 1]
            + terms[:, 2 * heads + h : 2 * heads + h + 1]
        )
        w = 1.0 / (1.0 + jnp.exp2(there - lse[:, h : h + 1]))
        o = own[:, at : at + NOPE] * w + got[:, at : at + NOPE].astype(f32) * (1.0 - w)
        at = part * wide + h * NOPE
        out[:, at : at + NOPE] = jnp.where(alive, o, 0.0).astype(bf16)
    if part:
        moving.wait()


def combine_first(starts, lens, own, lse, got, half, earlier):
    rows, wide = own.shape
    return pl.pallas_call(
        functools.partial(combine_kernel, rows, wide // NOPE, half, 0),
        out_shape=pltpu.VMEM((rows, 2 * wide), bf16),
        in_specs=[SMEM, SMEM] + [VMEM] * 3 + [ANY],
        out_specs=VMEM,
        compiler_params=params(2),
        cost_estimate=cost(8 * rows * wide),
    )(starts, lens, *held_in_vmem(own, lse, got, earlier))


def combine_second(starts, lens, own, lse, got, half, before, weights):
    rows, wide = own.shape
    return pl.pallas_call(
        functools.partial(combine_kernel, rows, wide // NOPE, half, 1),
        out_shape=(
            pltpu.VMEM((rows, 2 * wide), bf16),
            pltpu.VMEM(weights.shape, weights.dtype),
        ),
        in_specs=[SMEM, SMEM] + [VMEM] * 4 + [ANY],
        out_specs=(VMEM, ANY),
        scratch_shapes=[pltpu.SemaphoreType.DMA(())],
        input_output_aliases={5: 0},
        compiler_params=params(2),
        cost_estimate=cost(8 * rows * wide),
    )(starts, lens, *held_in_vmem(own, lse, got, before), weights)


NEAR = (0, 1, 2, 3, 5, 6, 7)


def products(pieces, weights, held):
    w00, w01, w10, w11 = weights
    depth = w00.shape[1]
    place = 0
    for piece in pieces:
        held[place : place + piece.shape[0], :] = piece[...]
        place += piece.shape[0]
    left = held[:, :depth]
    right = held[:, depth:]
    mine = nt(left, w00[...]) + nt(right, w10[...])
    other = nt(left, w01[...]) + nt(right, w11[...])
    swapped = lax.axis_index("yh") != lax.axis_index("yl")
    return jnp.concatenate(
        [jnp.where(swapped, other, mine), jnp.where(swapped, mine, other)], axis=1
    ).astype(bf16)


def near_kernel(rows, *refs):
    count = len(NEAR)
    out, held = refs[-2:]
    both = products(refs[:count], refs[count : count + 4], held)
    out[: 4 * rows, :] = both[: 4 * rows]
    out[5 * rows :, :] = both[4 * rows :]


def far_kernel(rows, *refs):
    outs = refs[7:15]
    full, held = refs[15:]
    full[4 * rows : 5 * rows, :] = products(refs[:2], refs[2:6], held)
    z, core, x = (lax.axis_index(name) for name in ("z", "core", "x"))
    odd = x & 1
    partners = (x, x + 1 - 2 * odd, (x - 1 + 2 * odd) & 3, (x + 2) & 3)
    for k, out in enumerate(outs):
        to_x, to_core = partners[k // 2], (core if k % 2 == 0 else 1 - core)
        slot = (z - 2 * to_x - to_core) & 7
        out[...] = full[pl.ds(pl.multiple_of(slot * rows, rows), rows), :]


def project_near(pieces, weights):
    rows, wide = pieces[0].shape
    cols = weights[0].shape[0]
    count = len(NEAR)
    return pl.pallas_call(
        functools.partial(near_kernel, rows),
        out_shape=pltpu.VMEM((8 * rows, 2 * cols), bf16),
        in_specs=[VMEM] * (count + 4),
        out_specs=VMEM,
        scratch_shapes=[pltpu.VMEM((count * rows, wide), bf16)],
        compiler_params=params(12),
        cost_estimate=cost(4 * count * rows * wide * cols),
    )(*held_in_vmem(*pieces, *weights))


def project_far(pieces, weights, near):
    wide = pieces[0].shape[1]
    cols = weights[0].shape[0]
    rows = near.shape[0] // 8
    block = pltpu.VMEM((rows, 2 * cols), bf16)
    return pl.pallas_call(
        functools.partial(far_kernel, rows),
        out_shape=(block,) * 8 + (pltpu.VMEM(near.shape, bf16),),
        in_specs=[VMEM] * 7,
        out_specs=(VMEM,) * 9,
        scratch_shapes=[pltpu.VMEM((rows, wide), bf16)],
        input_output_aliases={6: 8},
        compiler_params=params(12),
        cost_estimate=cost(4 * rows * wide * cols),
    )(*held_in_vmem(*pieces, *weights, near))


def level_kernel(*refs):
    pass


def level(arrays, earlier=()):
    count = len(arrays)
    return pl.pallas_call(
        level_kernel,
        out_shape=tuple(pltpu.VMEM(x.shape, x.dtype) for x in arrays),
        in_specs=[ANY] * (count + len(earlier)),
        out_specs=(ANY,) * count,
        input_output_aliases={i: i for i in range(count)},
        compiler_params=params(1),
    )(*held_in_vmem(*arrays, *earlier))


def swap(x, axis):
    return lax.ppermute(x, axis, [(0, 1), (1, 0)])


UP = [(i, (i + 1) % 8) for i in range(8)]
DOWN = [(i, (i - 1) % 8) for i in range(8)]


def step(a, b):
    return lax.ppermute(a, "z", UP), lax.ppermute(b, "z", DOWN)


def last(a, b):
    cut = a.shape[0] // 2
    return step(a[:cut], b[cut:])


X_PAIRS = ((1, 0, 3, 2), (3, 2, 1, 0), (2, 3, 0, 1))


def to_partner(x, pairs, flip):
    moves = [(2 * i + c, 2 * j + (c ^ flip)) for i, j in enumerate(pairs) for c in range(2)]
    return lax.ppermute(x, ("x", "core"), moves)


def pack_kernel(q_nope, q_rope, cache, stretch, w, latent, q_own, q_sent, w_near, sems):
    core = lax.axis_index("core")
    rows, wide = q_nope.shape[1:]
    moves = [
        (cache.at[core], latent.at[:rows, :]),
        (stretch.at[core], latent.at[rows:, :]),
        (q_nope.at[core], q_own.at[:, :wide]),
        (q_rope.at[core], q_own.at[:, wide:]),
        (q_nope.at[1 - core], q_sent.at[:, :wide]),
        (q_rope.at[1 - core], q_sent.at[:, wide:]),
        (w, w_near),
    ]
    copies = [pltpu.make_async_copy(a, b, sems.at[i]) for i, (a, b) in enumerate(moves)]
    for copy in copies:
        copy.start()
    for copy in copies:
        copy.wait()


def pack(q_nope, q_rope, cache, stretch, w):
    rows, width = cache.shape[1:]
    wide = q_nope.shape[2] + q_rope.shape[2]
    return pl.pallas_call(
        pack_kernel,
        out_shape=(
            pltpu.VMEM((2 * rows, width), bf16),
            pltpu.VMEM((rows, wide), bf16),
            pltpu.VMEM((rows, wide), bf16),
            pltpu.VMEM(w.shape, bf16),
        ),
        in_specs=[ANY] * 5,
        out_specs=(ANY,) * 4,
        scratch_shapes=[pltpu.SemaphoreType.DMA((7,))],
        compiler_params=params(1),
    )(*in_hbm(q_nope, q_rope, cache, stretch, w))


def sum_kernel(*refs):
    parts, (first, second) = refs[:8], refs[8:]
    core = lax.axis_index("core")
    cols = first.shape[2]
    for k in range(2):
        total = parts[4 * k][...].astype(f32)
        for part in parts[4 * k + 1 : 4 * k + 4]:
            total += part[...].astype(f32)
        total = total.astype(bf16)
        to = core if k == 0 else 1 - core
        first[to] = total[:, :cols]
        second[to] = total[:, cols:]


def sums(own_seq, other_seq):
    rows, cols = own_seq[0].shape
    out = pltpu.VMEM((2, rows, cols // 2), bf16)
    return pl.pallas_call(
        sum_kernel,
        out_shape=(out, out),
        in_specs=[VMEM] * 8,
        out_specs=(VMEM, VMEM),
        compiler_params=params(4),
    )(*held_in_vmem(*own_seq, *other_seq))


def local(q_nope, q_rope, cache_latent, stretch_latent, w_uk, w_uv, w_o, stretch_start, prompt_len):
    half = 8 * q_nope.shape[1]
    latent, q_own, q_sent, w_uk_near = pack(
        q_nope, q_rope, cache_latent, stretch_latent, w_uk
    )
    q_own_y = swap(q_own, "yl")
    q_got = swap(q_sent, "core")
    u1, d1, q_got = level((*step(latent, latent), q_got))
    u2, d2 = level(step(u1, d1))
    q_got_y = swap(q_got, "yl")
    w_uk2 = swap(w_uk, "core")
    w_uv2 = swap(w_uv, "core")
    near = [latent, u1, u2, d1]
    near_at, far_at = (0, 1, 2, 7), (6, 3, 5, 4)
    *a1, w_t = attention_first(
        stretch_start, q_own, q_own_y, w_uk_near, near, near_at, half, u1, w_o.T
    )
    u3, d3, w_t = level((*step(u2, d2), w_t), (q_got_y, w_uk2, w_uv2, a1[2]))
    w_t_c = swap(w_t, "core")
    b1 = attention_first(stretch_start, q_got, q_got_y, w_uk2, near, near_at, half, u3)
    far = [d2, u3, d3, *last(u3, d3)]
    a2 = attention_second(stretch_start, a1, w_uv, far, far_at, half, b1[2])
    got_a = swap(a2[2], "yl")
    b2 = attention_second(stretch_start, b1, w_uv2, far, far_at, half, a2[1], w_t_c)
    got_b = swap(b2[2], "yl")
    known = (stretch_start, prompt_len)
    attention = combine_first(*known, *a2[:2], got_a, half, b2[1])
    attention, w_t = combine_second(*known, *b2[:2], got_b, half, attention, w_o.T)

    u1, d1 = level(step(attention, attention))
    w_t_y = swap(w_t, "yl")
    u2, d2 = level(step(u1, d1))
    u3, d3, w_t_y = level((*step(u2, d2), w_t_y))
    w_t_cy = swap(w_t_y, "core")
    weights = (w_t, w_t_y, w_t_c, w_t_cy)
    near = project_near([attention, u1, u2, u3, d3, d2, d1], weights)
    parts = project_far(last(u3, d3), weights, near)

    other_seq = [swap(parts[1], "core")]
    other_seq += [to_partner(parts[2 * k + 3], X_PAIRS[k], 1) for k in range(3)]
    own_seq = [parts[0]] + [to_partner(parts[2 * k + 2], X_PAIRS[k], 0) for k in range(3)]
    first, second = sums(own_seq, other_seq)
    first = lax.ppermute(first, ("yl", "yh"), [(0, 0), (1, 2), (2, 1), (3, 3)])
    second = lax.ppermute(second, ("yl", "yh"), [(0, 2), (2, 3), (1, 0), (3, 1)])
    return (first.astype(f32) + second.astype(f32)).astype(bf16)


def solution(mesh):
    fine = Mesh(mesh.devices.reshape(2, 8, 2, 4, 2), ("yl", "z", "yh", "x", "core"))
    ctx = ("yl", "z")
    head = ("yh", "x", "core")
    placed = (
        P(None, ctx, head),
        P(None, ctx, head),
        P(None, ctx, None),
        P(None, ctx, None),
        P(None, head),
        P(None, head),
        P(head, ctx),
        P(),
        P(),
    )
    return jax.shard_map(
        local, mesh=fine, in_specs=placed, out_specs=P(None, head, ctx), check_vma=False
    )
```

```python
import functools

import jax
import jax.numpy as jnp
from jax import lax
from jax.experimental import pallas as pl
from jax.experimental.pallas import tpu as pltpu
from jax.sharding import Mesh, PartitionSpec as P

LATENT = 512
ROPE = 64
NOPE = 128
LOG2E = 1.4426950408889634
HIDDEN = -1e30
GROUP = 8
MIB = 1024 * 1024

f32 = jnp.float32
bf16 = jnp.bfloat16


def nt(a, b):
    return lax.dot_general(a, b, (((1,), (1,)), ((), ())), preferred_element_type=f32)


def nn(a, b):
    return jnp.dot(a, b, preferred_element_type=f32)


def load_keys(rows, slots, pieces, keys):
    place = 0
    for piece in pieces:
        height = piece.shape[0]
        value = piece[...]
        keys[place : place + height, :LATENT] = value[:, :LATENT]
        rope = value[:, LATENT:]
        keys[place : place + height, LATENT:] = jnp.concatenate([rope, rope], axis=1)
        place += height


def hidden_keys(rows, slots, half, starts):
    y, z = lax.axis_index("yl"), lax.axis_index("z")
    start = starts[lax.axis_index("core")]
    row = lax.broadcasted_iota(jnp.int32, (2 * rows, 2 * rows), 0)
    col = lax.broadcasted_iota(jnp.int32, (2 * rows, 2 * rows), 1)
    partner = (row >= rows).astype(jnp.int32)
    q_y = y + partner * (1 - 2 * y)
    q_pos = q_y * half + z * rows + row - partner * rows
    in_cache = col < rows
    limit = jnp.where(in_cache, start, q_pos + 1)
    inner = y * half + jnp.where(in_cache, col, col - rows)
    return jnp.concatenate(
        [
            jnp.where(inner + ((z - d) & 7) * rows < limit, 0.0, HIDDEN).astype(f32)
            for d in slots
        ],
        axis=1,
    )


def scores_of(q, keys, bias):
    s = nt(q, keys[...])
    height, count = bias.shape
    return (s.reshape(GROUP, height, count) + bias[...][None]).reshape(GROUP * height, count)


def tiled(x, like):
    return jnp.concatenate([x] * (like.shape[1] // 128), axis=1)


def first_kernel(rows, heads, half, slots, *refs):
    c = (NOPE + ROPE) ** -0.5 * LOG2E
    starts, q0, q1, wuk = refs[:4]
    pieces = refs[4 : 4 + len(slots)]
    rest = refs[5 + len(slots) :]
    moving = None
    if len(rest) > 5:
        moving = pltpu.make_async_copy(rest[0], rest[4], rest[-1])
        moving.start()
        rest = (*rest[1:4], *rest[5:7])
    qaug, acc, stats, keys, bias = rest
    load_keys(rows, slots, pieces, keys)
    bias[...] = hidden_keys(rows, slots, half, starts)
    wide = heads * NOPE
    block = GROUP * 2 * rows
    low = lax.broadcasted_iota(jnp.int32, (2 * rows, 2 * ROPE), 1) < ROPE
    for g in range(heads // GROUP):
        for j in range(GROUP):
            h = g * GROUP + j
            at = h * NOPE
            q = jnp.concatenate([q0[:, at : at + NOPE], q1[:, at : at + NOPE]], axis=0)
            r0 = wide + (h // 2) * 2 * ROPE
            r = jnp.concatenate([q0[:, r0 : r0 + 2 * ROPE], q1[:, r0 : r0 + 2 * ROPE]], axis=0)
            keep = low if h % 2 == 0 else jnp.logical_not(low)
            base = h * 2 * rows
            qaug[base : base + 2 * rows, :LATENT] = nt(q, wuk[:, at : at + NOPE]).astype(bf16)
            qaug[base : base + 2 * rows, LATENT:] = jnp.where(keep, r, jnp.zeros_like(r))
        here = slice(g * block, (g + 1) * block)
        s = scores_of(qaug[here], keys, bias)
        m = jnp.broadcast_to(jnp.max(s, axis=-1, keepdims=True), (block, 128))
        p = jnp.exp2((s - tiled(m, s)) * c)
        acc[here] = nn(p.astype(bf16), keys[:, :LATENT])
        stats[here, :128] = m
        stats[here, 128:] = jnp.broadcast_to(jnp.sum(p, axis=-1, keepdims=True), (block, 128))
    if moving is not None:
        moving.wait()


def second_kernel(rows, heads, half, slots, *refs):
    c = (NOPE + ROPE) ** -0.5 * LOG2E
    starts, qaug, acc, stats, wuv = refs[:5]
    pieces = refs[5 : 6 + len(slots)]
    own, own_lse, message, keys, bias = refs[-5:]
    load_keys(rows, slots, pieces, keys)
    bias[...] = hidden_keys(rows, slots, half, starts)
    wide = heads * NOPE
    block = GROUP * 2 * rows
    out_lane = lax.broadcasted_iota(jnp.int32, (rows, 128), 1)
    own_all = jnp.zeros((rows, 128), f32)
    sent_all = jnp.zeros((rows, 128), f32)
    for g in range(heads // GROUP):
        here = slice(g * block, (g + 1) * block)
        s = scores_of(qaug[here], keys, bias)
        m1 = stats[here, :128]
        m = jnp.maximum(m1, jnp.max(s, axis=-1, keepdims=True))
        factor = jnp.exp2((m1 - m) * c)
        p = jnp.exp2((s - tiled(m, s)) * c)
        total = stats[here, 128:] * factor + jnp.sum(p, axis=-1, keepdims=True)
        fresh = nn(p.astype(bf16), keys[:, :LATENT])
        inverse = 1.0 / total
        mixed = acc[here] * tiled(factor * inverse, fresh) + fresh * tiled(inverse, fresh)
        mixed = mixed.astype(bf16)
        lse = m * c + jnp.log2(total)
        for j in range(GROUP):
            h = g * GROUP + j
            at = h * NOPE
            base = j * 2 * rows
            o = nn(mixed[base : base + 2 * rows], wuv[:, at : at + NOPE])
            own[:, at : at + NOPE] = o[:rows]
            message[:, at : at + NOPE] = o[rows:].astype(bf16)
            own_all = jnp.where(out_lane == h, lse[base : base + rows], own_all)
            rest = lse[base + rows : base + 2 * rows]
            for term in range(3):
                part = rest.astype(bf16).astype(f32)
                sent_all = jnp.where(out_lane == term * heads + h, part, sent_all)
                rest = rest - part
    own_lse[...] = own_all
    message[:, wide : wide + 128] = sent_all.astype(bf16)


VMEM = pl.BlockSpec(memory_space=pltpu.VMEM)
SMEM = pl.BlockSpec(memory_space=pltpu.SMEM)
ANY = pl.BlockSpec(memory_space=pl.ANY)


def params(mib):
    return pltpu.CompilerParams(vmem_limit_bytes=mib * MIB)


def held_in_vmem(*arrays):
    return tuple(pltpu.with_memory_space_constraint(x, pltpu.VMEM) for x in arrays)


def in_hbm(*arrays):
    return tuple(pltpu.with_memory_space_constraint(x, pltpu.HBM) for x in arrays)


def cost(flops, exps=0):
    return pl.CostEstimate(flops=flops, transcendentals=exps, bytes_accessed=4 * MIB)


def attention_first(starts, q0, q1, wuk, pieces, slots, half, earlier, weights=None):
    rows = q0.shape[0]
    heads = wuk.shape[1] // NOPE
    height = heads * 2 * rows
    count = 2 * rows * len(slots)
    carried = () if weights is None else in_hbm(weights)
    return pl.pallas_call(
        functools.partial(first_kernel, rows, heads, half, slots),
        out_shape=(
            pltpu.VMEM((height, LATENT + 2 * ROPE), bf16),
            pltpu.VMEM((height, LATENT), f32),
            pltpu.VMEM((height, 256), f32),
            *(pltpu.VMEM(x.shape, bf16) for x in carried),
        ),
        in_specs=[SMEM] + [VMEM] * (3 + len(pieces)) + [ANY] * (1 + len(carried)),
        out_specs=(VMEM,) * 3 + (ANY,) * len(carried),
        scratch_shapes=[
            pltpu.VMEM((count, LATENT + 2 * ROPE), bf16),
            pltpu.VMEM((2 * rows, count), f32),
        ]
        + [pltpu.SemaphoreType.DMA(())] * len(carried),
        compiler_params=params(16),
        cost_estimate=cost(2 * height * count * (2 * LATENT + 2 * ROPE), height * count),
    )(starts, *held_in_vmem(q0, q1, wuk, *pieces, earlier), *carried)


def attention_second(starts, state, wuv, pieces, slots, half, *earlier):
    heads = wuv.shape[1] // NOPE
    height = state[0].shape[0]
    rows = height // heads // 2
    count = 2 * rows * len(slots)
    wide = heads * NOPE
    return pl.pallas_call(
        functools.partial(second_kernel, rows, heads, half, slots),
        out_shape=(
            pltpu.VMEM((rows, wide), f32),
            pltpu.VMEM((rows, 128), f32),
            pltpu.VMEM((rows, wide + 128), bf16),
        ),
        in_specs=[SMEM] + [VMEM] * (4 + len(pieces)) + [ANY] * len(earlier),
        out_specs=(VMEM, VMEM, VMEM),
        scratch_shapes=[
            pltpu.VMEM((count, LATENT + 2 * ROPE), bf16),
            pltpu.VMEM((2 * rows, count), f32),
        ],
        compiler_params=params(16),
        cost_estimate=cost(2 * height * count * (2 * LATENT + 2 * ROPE), height * count),
    )(starts, *held_in_vmem(*state, wuv, *pieces, *earlier))


def combine_kernel(rows, heads, half, part, starts, lens, own, lse, got, *refs):
    out = refs[-1 - 2 * part]
    if part:
        weights, (copied, sem) = refs[-4], refs[-2:]
        moving = pltpu.make_async_copy(weights, copied, sem)
        moving.start()
    core = lax.axis_index("core")
    live = lens[core] - starts[core]
    base = lax.axis_index("yl") * half + lax.axis_index("z") * rows
    wide = heads * NOPE
    alive = base + lax.broadcasted_iota(jnp.int32, (rows, 1), 0) < live
    terms = got[:, wide : wide + 128].astype(f32)
    for h in range(heads):
        at = h * NOPE
        there = (
            terms[:, h : h + 1]
            + terms[:, heads + h : heads + h + 1]
            + terms[:, 2 * heads + h : 2 * heads + h + 1]
        )
        w = 1.0 / (1.0 + jnp.exp2(there - lse[:, h : h + 1]))
        o = own[:, at : at + NOPE] * w + got[:, at : at + NOPE].astype(f32) * (1.0 - w)
        at = part * wide + h * NOPE
        out[:, at : at + NOPE] = jnp.where(alive, o, 0.0).astype(bf16)
    if part:
        moving.wait()


def combine_first(starts, lens, own, lse, got, half, earlier):
    rows, wide = own.shape
    return pl.pallas_call(
        functools.partial(combine_kernel, rows, wide // NOPE, half, 0),
        out_shape=pltpu.VMEM((rows, 2 * wide), bf16),
        in_specs=[SMEM, SMEM] + [VMEM] * 3 + [ANY],
        out_specs=VMEM,
        compiler_params=params(2),
        cost_estimate=cost(8 * rows * wide),
    )(starts, lens, *held_in_vmem(own, lse, got, earlier))


def combine_second(starts, lens, own, lse, got, half, before, weights):
    rows, wide = own.shape
    return pl.pallas_call(
        functools.partial(combine_kernel, rows, wide // NOPE, half, 1),
        out_shape=(
            pltpu.VMEM((rows, 2 * wide), bf16),
            pltpu.VMEM(weights.shape, weights.dtype),
        ),
        in_specs=[SMEM, SMEM] + [VMEM] * 4 + [ANY],
        out_specs=(VMEM, ANY),
        scratch_shapes=[pltpu.SemaphoreType.DMA(())],
        input_output_aliases={5: 0},
        compiler_params=params(2),
        cost_estimate=cost(8 * rows * wide),
    )(starts, lens, *held_in_vmem(own, lse, got, before), weights)


NEAR = (0, 1, 2, 3, 5, 6, 7)


def products(pieces, weights, held):
    w00, w01, w10, w11 = weights
    depth = w00.shape[1]
    place = 0
    for piece in pieces:
        held[place : place + piece.shape[0], :] = piece[...]
        place += piece.shape[0]
    left = held[:, :depth]
    right = held[:, depth:]
    mine = nt(left, w00[...]) + nt(right, w10[...])
    other = nt(left, w01[...]) + nt(right, w11[...])
    swapped = lax.axis_index("yh") != lax.axis_index("yl")
    return jnp.concatenate(
        [jnp.where(swapped, other, mine), jnp.where(swapped, mine, other)], axis=1
    ).astype(bf16)


def near_kernel(rows, *refs):
    count = len(NEAR)
    out, held = refs[-2:]
    both = products(refs[:count], refs[count : count + 4], held)
    out[: 4 * rows, :] = both[: 4 * rows]
    out[5 * rows :, :] = both[4 * rows :]


def far_kernel(rows, *refs):
    outs = refs[7:15]
    full, held = refs[15:]
    full[4 * rows : 5 * rows, :] = products(refs[:2], refs[2:6], held)
    z, core, x = (lax.axis_index(name) for name in ("z", "core", "x"))
    odd = x & 1
    partners = (x, x + 1 - 2 * odd, (x - 1 + 2 * odd) & 3, (x + 2) & 3)
    for k, out in enumerate(outs):
        to_x, to_core = partners[k // 2], (core if k % 2 == 0 else 1 - core)
        slot = (z - 2 * to_x - to_core) & 7
        out[...] = full[pl.ds(pl.multiple_of(slot * rows, rows), rows), :]


def project_near(pieces, weights):
    rows, wide = pieces[0].shape
    cols = weights[0].shape[0]
    count = len(NEAR)
    return pl.pallas_call(
        functools.partial(near_kernel, rows),
        out_shape=pltpu.VMEM((8 * rows, 2 * cols), bf16),
        in_specs=[VMEM] * (count + 4),
        out_specs=VMEM,
        scratch_shapes=[pltpu.VMEM((count * rows, wide), bf16)],
        compiler_params=params(12),
        cost_estimate=cost(4 * count * rows * wide * cols),
    )(*held_in_vmem(*pieces, *weights))


def project_far(pieces, weights, near):
    wide = pieces[0].shape[1]
    cols = weights[0].shape[0]
    rows = near.shape[0] // 8
    block = pltpu.VMEM((rows, 2 * cols), bf16)
    return pl.pallas_call(
        functools.partial(far_kernel, rows),
        out_shape=(block,) * 8 + (pltpu.VMEM(near.shape, bf16),),
        in_specs=[VMEM] * 7,
        out_specs=(VMEM,) * 9,
        scratch_shapes=[pltpu.VMEM((rows, wide), bf16)],
        input_output_aliases={6: 8},
        compiler_params=params(12),
        cost_estimate=cost(4 * rows * wide * cols),
    )(*held_in_vmem(*pieces, *weights, near))


def level_kernel(*refs):
    pass


def level(arrays, earlier=()):
    count = len(arrays)
    return pl.pallas_call(
        level_kernel,
        out_shape=tuple(pltpu.VMEM(x.shape, x.dtype) for x in arrays),
        in_specs=[ANY] * (count + len(earlier)),
        out_specs=(ANY,) * count,
        input_output_aliases={i: i for i in range(count)},
        compiler_params=params(1),
    )(*held_in_vmem(*arrays, *earlier))


def swap(x, axis):
    return lax.ppermute(x, axis, [(0, 1), (1, 0)])


UP = [(i, (i + 1) % 8) for i in range(8)]
DOWN = [(i, (i - 1) % 8) for i in range(8)]


def step(a, b):
    return lax.ppermute(a, "z", UP), lax.ppermute(b, "z", DOWN)


def last(a, b):
    cut = a.shape[0] // 2
    return step(a[:cut], b[cut:])


X_PAIRS = ((1, 0, 3, 2), (3, 2, 1, 0), (2, 3, 0, 1))


def to_partner(x, pairs, flip):
    moves = [(2 * i + c, 2 * j + (c ^ flip)) for i, j in enumerate(pairs) for c in range(2)]
    return lax.ppermute(x, ("x", "core"), moves)


def pack_kernel(q_nope, q_rope, cache, stretch, w, latent, q_own, q_sent, w_near, sems):
    core = lax.axis_index("core")
    rows, wide = q_nope.shape[1:]
    moves = [
        (cache.at[core], latent.at[:rows, :]),
        (stretch.at[core], latent.at[rows:, :]),
        (q_nope.at[core], q_own.at[:, :wide]),
        (q_rope.at[core], q_own.at[:, wide:]),
        (q_nope.at[1 - core], q_sent.at[:, :wide]),
        (q_rope.at[1 - core], q_sent.at[:, wide:]),
        (w, w_near),
    ]
    copies = [pltpu.make_async_copy(a, b, sems.at[i]) for i, (a, b) in enumerate(moves)]
    for copy in copies:
        copy.start()
    for copy in copies:
        copy.wait()


def pack(q_nope, q_rope, cache, stretch, w):
    rows, width = cache.shape[1:]
    wide = q_nope.shape[2] + q_rope.shape[2]
    return pl.pallas_call(
        pack_kernel,
        out_shape=(
            pltpu.VMEM((2 * rows, width), bf16),
            pltpu.VMEM((rows, wide), bf16),
            pltpu.VMEM((rows, wide), bf16),
            pltpu.VMEM(w.shape, bf16),
        ),
        in_specs=[ANY] * 5,
        out_specs=(ANY,) * 4,
        scratch_shapes=[pltpu.SemaphoreType.DMA((7,))],
        compiler_params=params(1),
    )(*in_hbm(q_nope, q_rope, cache, stretch, w))


def sum_kernel(*refs):
    parts, (first, second) = refs[:8], refs[8:]
    core = lax.axis_index("core")
    cols = first.shape[2]
    for k in range(2):
        total = parts[4 * k][...].astype(f32)
        for part in parts[4 * k + 1 : 4 * k + 4]:
            total += part[...].astype(f32)
        total = total.astype(bf16)
        to = core if k == 0 else 1 - core
        first[to] = total[:, :cols]
        second[to] = total[:, cols:]


def sums(own_seq, other_seq):
    rows, cols = own_seq[0].shape
    out = pltpu.VMEM((2, rows, cols // 2), bf16)
    return pl.pallas_call(
        sum_kernel,
        out_shape=(out, out),
        in_specs=[VMEM] * 8,
        out_specs=(VMEM, VMEM),
        compiler_params=params(4),
    )(*held_in_vmem(*own_seq, *other_seq))


def local(q_nope, q_rope, cache_latent, stretch_latent, w_uk, w_uv, w_o, stretch_start, prompt_len):
    half = 8 * q_nope.shape[1]
    latent, q_own, q_sent, w_uk_near = pack(
        q_nope, q_rope, cache_latent, stretch_latent, w_uk
    )
    q_own_y = swap(q_own, "yl")
    q_got = swap(q_sent, "core")
    u1, d1, q_got = level((*step(latent, latent), q_got))
    u2, d2 = level(step(u1, d1))
    q_got_y = swap(q_got, "yl")
    w_uk2 = swap(w_uk, "core")
    w_uv2 = swap(w_uv, "core")
    near = [latent, u1, u2, d1]
    near_at, far_at = (0, 1, 2, 7), (6, 3, 5, 4)
    *a1, w_t = attention_first(
        stretch_start, q_own, q_own_y, w_uk_near, near, near_at, half, u1, w_o.T
    )
    u3, d3, w_t = level((*step(u2, d2), w_t), (q_got_y, w_uk2, w_uv2, a1[2]))
    w_t_c = swap(w_t, "core")
    b1 = attention_first(stretch_start, q_got, q_got_y, w_uk2, near, near_at, half, u3)
    far = [d2, u3, d3, *last(u3, d3)]
    a2 = attention_second(stretch_start, a1, w_uv, far, far_at, half, b1[2])
    got_a = swap(a2[2], "yl")
    b2 = attention_second(stretch_start, b1, w_uv2, far, far_at, half, a2[1], w_t_c)
    got_b = swap(b2[2], "yl")
    known = (stretch_start, prompt_len)
    attention = combine_first(*known, *a2[:2], got_a, half, b2[1])
    attention, w_t = combine_second(*known, *b2[:2], got_b, half, attention, w_o.T)

    u1, d1 = level(step(attention, attention))
    w_t_y = swap(w_t, "yl")
    u2, d2 = level(step(u1, d1))
    u3, d3, w_t_y = level((*step(u2, d2), w_t_y))
    w_t_cy = swap(w_t_y, "core")
    weights = (w_t, w_t_y, w_t_c, w_t_cy)
    near = project_near([attention, u1, u2, u3, d3, d2, d1], weights)
    parts = project_far(last(u3, d3), weights, near)

    other_seq = [swap(parts[1], "core")]
    other_seq += [to_partner(parts[2 * k + 3], X_PAIRS[k], 1) for k in range(3)]
    own_seq = [parts[0]] + [to_partner(parts[2 * k + 2], X_PAIRS[k], 0) for k in range(3)]
    first, second = sums(own_seq, other_seq)
    kept = lax.axis_index("yl") == lax.axis_index("yh")
    first = jnp.where(kept, first, lax.ppermute(first, ("yl", "yh"), [(1, 2), (2, 1)]))
    second = lax.ppermute(second, ("yl", "yh"), [(0, 2), (2, 3), (1, 0), (3, 1)])
    return (first.astype(f32) + second.astype(f32)).astype(bf16)


def solution(mesh):
    fine = Mesh(mesh.devices.reshape(2, 8, 2, 4, 2), ("yl", "z", "yh", "x", "core"))
    ctx = ("yl", "z")
    head = ("yh", "x", "core")
    placed = (
        P(None, ctx, head),
        P(None, ctx, head),
        P(None, ctx, None),
        P(None, ctx, None),
        P(None, head),
        P(None, head),
        P(head, ctx),
        P(),
        P(),
    )
    return jax.shard_map(
        local, mesh=fine, in_specs=placed, out_specs=P(None, head, ctx), check_vma=False
    )
```
